512 devices in a mesh: space: 128 (over z_lo, x, y, core), case: 4 (over z_hi).
Axes of the slice: x: 4, y: 4, z: 16 (z_hi: 4, z_lo: 4; z = z_hi * 4 + z_lo), core: 2. Of those that a mesh axis runs over, the one named last changes fastest.
Arguments:
- spectrum: float32 [4, 36, 32, 16384], P('case', None, None, 'space'), may hold values from 0.25 to 7.5, as said below
- cotangent: float32 [4, 36, 32, 16384], P('case', None, None, 'space'), may hold values from -6 to 6
- courant: float32 [36, 16384], P(None, 'space'), may hold values from 0.05 to 0.9
- upwind: int32 [36, 16384], P(None, 'space'), may hold values from 0 to 255, as said below
- w_in: bfloat16 [32, 128], replicated, may hold values from -1 to 1
- b_in: float32 [128], replicated, may hold values from -3 to 3
- w_mid: bfloat16 [128, 128], replicated, may hold values from -0.5 to 0.5
- b_mid: float32 [128], replicated, may hold values from -3 to 3
- w_out: bfloat16 [128, 32], replicated, may hold values from -0.5 to 0.5
- b_out: float32 [32], replicated, may hold values from -3 to 3
Outputs:
- state_grad: float32 [4, 36, 32, 16384], P('case', None, None, 'space')
- grad_w_in: float32 [32, 128], replicated
- grad_b_in: float32 [128], replicated
- grad_w_mid: float32 [128, 128], replicated
- grad_b_mid: float32 [128], replicated
- grad_w_out: float32 [128, 32], replicated
- grad_b_out: float32 [32], replicated
The draws below stay inside these ranges and needn't reach their ends.
Inputs may be any that keep to these rules, and one draw needn't show every extreme that they name: `spectrum`: positive spectral densities. `upwind`: an index into a device's own 128 nodes extended by 64 nodes on each side: value i stands for node i - 64 of the device's block. It lies within 64 of the node's own extended index and never equals it.
All inputs are finite; a program needn't handle non-finite values.
Results may differ from the reference program's by a relative error of at most 0.0065.
The reference program's roundings to bfloat16 on the way count: a program that leaves them out, or rounds other values in their place, can miss the bound.
Values sent between devices are 32-bit elements; how exact they have to be, the bound alone decides.
No kernel may reach another device: no remote copies, remote signals or barrier semaphores. Data moves between devices by JAX's collectives and lax.ppermute only.
A program may use at most 64 MiB of HBM per device.

```python
import math
import jax
import jax.numpy as jnp
from jax import lax

DIRS = 36
FREQS = 32
HID = 128
HALO = 64
NODES_DEV = 128
NODES = 16384
CASES = 4


def draw_spectrum(key, part):
    key = jax.random.fold_in(key, 11)
    shape = (CASES, DIRS, FREQS, NODES)
    position = jnp.arange(NODES, dtype=jnp.float32) / jnp.float32(max(NODES - 1, 1))
    scale = 1.0 + 2.0 * position
    values = jnp.exp(jax.random.uniform(key, shape, jnp.float32, -1.0, 0.9))
    return values * scale


def draw_upwind(key, part):
    key = jax.random.fold_in(key, 23)
    key_mag, key_sign = jax.random.split(key)
    shape = (DIRS, NODES)
    magnitude = jax.random.randint(key_mag, shape, 1, HALO + 1)
    direction = jax.random.randint(key_sign, shape, 0, 2) * 2 - 1
    local = jnp.arange(NODES, dtype=jnp.int32)[None, :] % NODES_DEV
    dir_ids = jnp.arange(DIRS, dtype=jnp.int32)[:, None]
    offset = magnitude * direction
    offset = jnp.where((local == 0) & (dir_ids == 0), -HALO, offset)
    offset = jnp.where((local == NODES_DEV - 1) & (dir_ids == 0), HALO, offset)
    return (local + HALO + offset).astype(jnp.int32)


def shard_levels(stream_key, dims, cuts, least, high):
    def one(axis_at, blocks):
        steps = jax.random.uniform(jax.random.fold_in(jax.random.fold_in(stream_key, 6), axis_at), (blocks,), jnp.float32, least / len(cuts), high / len(cuts))
        return jnp.repeat(jnp.exp(steps), dims[axis_at] // blocks).reshape((-1,) + (1,) * (len(dims) - axis_at - 1))

    factor_of = one(*cuts[0])
    for cut in cuts[1:]:
        factor_of = factor_of * one(*cut)
    return factor_of


def normal_values(own_key, extent, deviation, most, cuts=(), kind=jnp.bfloat16):
    loudness = shard_levels(own_key, extent, cuts, -0.22, 0.18) if cuts else 1.0
    result = jax.random.normal(own_key, extent, jnp.float32) * deviation * loudness
    return jnp.minimum(jnp.maximum(result, -most), most).astype(kind)


def setup_inputs(seed: int = 0) -> dict:
    streams_of = jax.random.split(jax.random.key(seed), 11)
    spectrum = draw_spectrum(jax.random.fold_in(streams_of[10], 71), 0)
    cotangent = normal_values(streams_of[1], (CASES, DIRS, FREQS, NODES), 1.0, 6.0, ((0, 4), (3, 128)), jnp.float32)
    courant = jnp.clip(jnp.exp(math.log(0.9) - 2.8903717 * jax.random.uniform(streams_of[2], (DIRS, NODES), jnp.float32) ** shard_levels(streams_of[2], (DIRS, NODES), ((1, 128),), -0.2, 0.2)), 0.05, 0.9)
    upwind = draw_upwind(jax.random.fold_in(streams_of[10], 71), 0)
    w_in = normal_values(streams_of[4], (FREQS, HID), FREQS ** -0.5, 1.0)
    b_in = normal_values(streams_of[5], (HID,), 0.5, 3.0, (), jnp.float32)
    w_mid = normal_values(streams_of[6], (HID, HID), HID ** -0.5, 0.5)
    b_mid = normal_values(streams_of[7], (HID,), 0.5, 3.0, (), jnp.float32)
    w_out = normal_values(streams_of[8], (HID, FREQS), HID ** -0.5, 0.5)
    b_out = normal_values(streams_of[9], (FREQS,), 0.5, 3.0, (), jnp.float32)
    return {"spectrum": spectrum, "cotangent": cotangent, "courant": courant, "upwind": upwind, "w_in": w_in, "b_in": b_in, "w_mid": w_mid, "b_mid": b_mid, "w_out": w_out, "b_out": b_out}


time_step = 0.3
clip_norm = 100.0

def silu_slope(pre):
    logistic = jax.nn.sigmoid(pre)
    return logistic * (1.0 + pre * (1.0 - logistic))

def mlp_rows(values, weights):
    w_in, b_in, w_mid, b_mid, w_out, b_out = weights
    rounded = values.astype(jnp.bfloat16)
    pre_one = jnp.dot(w_in.T, rounded, preferred_element_type=jnp.float32) + b_in[:, None]
    act_one = jax.nn.silu(pre_one).astype(jnp.bfloat16)
    pre_two = jnp.dot(w_mid.T, act_one, preferred_element_type=jnp.float32) + b_mid[:, None]
    act_two = jax.nn.silu(pre_two).astype(jnp.bfloat16)
    source = jnp.dot(w_out.T, act_two, preferred_element_type=jnp.float32) + b_out[:, None]
    return (rounded, pre_one, act_one, pre_two, act_two, source)

def mlp_back(values, incoming, weights):
    w_in, b_in, w_mid, b_mid, w_out, b_out = weights
    rounded, pre_one, act_one, pre_two, act_two, source = mlp_rows(values, weights)
    g_source = (-time_step * incoming * values * jax.nn.sigmoid(source)).astype(jnp.bfloat16)
    grad_w_out = jnp.dot(act_two, g_source.T, preferred_element_type=jnp.float32)
    grad_b_out = lax.optimization_barrier(jnp.sum(g_source.astype(jnp.float32), axis=1))
    back_two = (jnp.dot(w_out, g_source, preferred_element_type=jnp.float32) * silu_slope(pre_two)).astype(jnp.bfloat16)
    grad_w_mid = jnp.dot(act_one, back_two.T, preferred_element_type=jnp.float32)
    grad_b_mid = lax.optimization_barrier(jnp.sum(back_two.astype(jnp.float32), axis=1))
    back_one = (jnp.dot(w_mid, back_two, preferred_element_type=jnp.float32) * silu_slope(pre_one)).astype(jnp.bfloat16)
    grad_w_in = jnp.dot(rounded, back_one.T, preferred_element_type=jnp.float32)
    grad_b_in = lax.optimization_barrier(jnp.sum(back_one.astype(jnp.float32), axis=1))
    back_state = jnp.dot(w_in, back_one, preferred_element_type=jnp.float32)
    gradients = (grad_w_in, grad_b_in, grad_w_mid, grad_b_mid, grad_w_out, grad_b_out)
    return (back_state, jax.nn.softplus(source), gradients)

def reference(spectrum, cotangent, courant, upwind, w_in, b_in, w_mid, b_mid, w_out, b_out):
    weights = (w_in, b_in, w_mid, b_mid, w_out, b_out)
    node_ids = jnp.arange(NODES, dtype=jnp.int32)
    block_start = node_ids // NODES_DEV * NODES_DEV
    neighbor = block_start[None, :] + upwind - HALO
    inside = (neighbor >= 0) & (neighbor < NODES)
    neighbor = jnp.where(inside, neighbor, NODES).astype(jnp.int32)
    column_index = jnp.broadcast_to(neighbor[:, None, :], (DIRS, FREQS, NODES))
    courant_b = courant[:, None, :]
    dir_ids = jnp.arange(DIRS, dtype=jnp.int32)[:, None, None]
    freq_ids = jnp.arange(FREQS, dtype=jnp.int32)[None, :, None]

    def back_step(field, incoming):

        def scan_fn(running, sliced):
            back_state, damping, gradients = mlp_back(sliced[0], sliced[1], weights)
            return (tuple((a + b for a, b in zip(running, gradients))), (back_state, damping))
        zeros = (jnp.zeros((FREQS, HID), jnp.float32), jnp.zeros((HID,), jnp.float32), jnp.zeros((HID, HID), jnp.float32), jnp.zeros((HID,), jnp.float32), jnp.zeros((HID, FREQS), jnp.float32), jnp.zeros((FREQS,), jnp.float32))
        running, (back_state, damping) = lax.scan(scan_fn, zeros, (field, incoming))
        spread = jnp.zeros((DIRS, FREQS, NODES + 1), jnp.float32).at[dir_ids, freq_ids, column_index].add(courant_b * incoming)
        outgoing = incoming * (1.0 - courant_b - time_step * damping) + back_state + spread[:, :, :NODES]
        return (outgoing, running)

    def one_case(pair_in):
        field, incoming = pair_in
        damping = lax.map(lambda rows: jax.nn.softplus(mlp_rows(rows, weights)[5]), field)
        padded = jnp.pad(field, ((0, 0), (0, 0), (0, 1)))
        upstream = jnp.take_along_axis(padded, column_index, axis=2)
        field_next = field - courant_b * (field - upstream) - time_step * damping * field
        grad_mid, later = back_step(field_next, incoming)
        grad_first, earlier = back_step(field, grad_mid)
        return (grad_first, tuple((a + b for a, b in zip(later, earlier))))
    state_grad, stacked = lax.map(one_case, (spectrum, cotangent))
    totals = tuple((lax.optimization_barrier(jnp.sum(part, axis=0)) for part in stacked))
    squares = jnp.float32(0.0)
    for part in totals:
        squares = squares + jnp.sum(part * part)
    factor = clip_norm / jnp.maximum(jnp.sqrt(squares), clip_norm)
    return (state_grad, totals[0] * factor, totals[1] * factor, totals[2] * factor, totals[3] * factor, totals[4] * factor, totals[5] * factor)
```

```python
import jax
import jax.numpy as jnp
import numpy as np
from jax import lax
from jax.experimental import pallas as pl
from jax.experimental.pallas import tpu as pltpu
from jax.sharding import PartitionSpec as P

DIRS = 36
FREQS = 32
HID = 128
HALO = 64
WIDTH = 128
TAIL = 48
CHUNK = 12
BLOCK = 12
ROWS = 256

time_step = 0.3
clip_norm = 100.0
F32 = jnp.float32
BF16 = jnp.bfloat16
LIMIT = 40 * 1024 * 1024


def dot(a, b):
    return jnp.dot(a, b, preferred_element_type=F32)


def dot_nt(a, b):
    return lax.dot_general(a, b, (((1,), (1,)), ((), ())), preferred_element_type=F32)


def lanes(shape):
    return lax.broadcasted_iota(jnp.int32, shape, len(shape) - 1)


def turned(x):
    return pltpu.roll(x, HALO, x.ndim - 1)


def low_lanes(a, b):
    return jnp.where(lanes(a.shape) < HALO, a, b)


def in_hbm(*arrays):
    return [pltpu.with_memory_space_constraint(x, pltpu.HBM) for x in arrays]


def is_odd():
    return lax.axis_index("space") % 2 == 1


def pack_kernel(spec, cot, courant, upwind, far, near):
    main = DIRS * FREQS
    sides = lanes((8, WIDTH)) < HALO
    mine = jnp.where(is_odd(), sides.astype(jnp.int32), 1 - sides.astype(jnp.int32))

    def put(rows, x, g):
        here = jnp.broadcast_to(mine[:1], x.shape) == 1
        x = turned(x)
        far[rows] = jnp.where(here, x, g)
        near[rows] = jnp.where(here, g, x)

    put(slice(0, main), spec[0].reshape(main, WIDTH), cot[0].reshape(main, WIDTH))
    put(slice(main, main + DIRS), upwind[...].astype(F32), courant[...])
    rest = jnp.zeros((TAIL - DIRS, WIDTH), F32)
    far[main + DIRS :] = rest
    near[main + DIRS :] = rest


def packed_halo(spectrum, cotangent, courant, upwind):
    out = jax.ShapeDtypeStruct((DIRS * FREQS + TAIL, WIDTH), F32)
    return pl.pallas_call(
        pack_kernel,
        out_shape=(out, out),
        compiler_params=pltpu.CompilerParams(vmem_limit_bytes=LIMIT),
        name="pack_halo",
    )(*in_hbm(spectrum, cotangent, courant, upwind))


def set_rim(far, near, rim_c, rim_u):
    odd = is_odd()
    below = jnp.where(odd, near[...], far[...])
    above = jnp.where(odd, far[...], near[...])
    rim_c[...] = low_lanes(above, below)
    own = turned(low_lanes(below, above))
    offset = jnp.where(lanes(own.shape) < HALO, WIDTH - HALO, -(HALO + WIDTH))
    rim_u[...] = own.astype(jnp.int32) + offset


def one_hot(target):
    place = lax.broadcasted_iota(jnp.int32, (WIDTH, WIDTH), 0)
    return jnp.where(place == target, 1.0, 0.0).astype(BF16)


def spread(value, hot):
    high = value.astype(BF16)
    low = (value - high.astype(F32)).astype(BF16)
    both = dot_nt(jnp.concatenate([high, low], axis=0), hot)
    return both[:FREQS] + both[FREQS:]


def gathered(x, index):
    return jnp.take_along_axis(x, index & (WIDTH - 1), axis=1, mode="promise_in_bounds")


def from_inside(index):
    return (index >= HALO) & (index < HALO + WIDTH)


def column(row):
    return jnp.broadcast_to(row, (HID, HID)).T


def wide(tile, width):
    return jnp.concatenate([tile] * (width // tile.shape[1]), axis=1)


def activated(pre):
    logistic = 0.5 + 0.5 * jnp.tanh(0.5 * pre)
    act = pre * logistic
    return act.astype(BF16), logistic + act * (1.0 - logistic)


def forward(x, w_in_t, b_in, w_mid_t, b_mid, w_out_t, b_out):
    width = x.shape[1]
    rounded = x.astype(BF16)
    act_one, slope_one = activated(dot(w_in_t, rounded) + wide(b_in, width))
    act_two, slope_two = activated(dot(w_mid_t, act_one) + wide(b_mid, width))
    source = dot(w_out_t, act_two) + wide(b_out, width)
    damping = jnp.maximum(source, 0.0) + jnp.log(1.0 + jnp.exp(-jnp.abs(source)))
    logistic = 0.5 + 0.5 * jnp.tanh(0.5 * source)
    return rounded, act_one, slope_one, act_two, slope_two, damping, logistic


def set_weights(w_in, b_in, w_mid, b_mid, w_out_t, b_out, w_in_t, b_in_c, w_mid_t, b_mid_c, b_out_c, w_out=None):
    w_in_t[...] = w_in[...].astype(F32).T.astype(BF16)
    w_mid_t[...] = w_mid[...].astype(F32).T.astype(BF16)
    b_in_c[...] = column(b_in[...])
    b_mid_c[...] = column(b_mid[...])
    row = jnp.broadcast_to(b_out[...], (HID, FREQS))
    b_out_c[...] = row.T
    if w_out is not None:
        w_out[...] = w_out_t[...].astype(F32).T.astype(BF16)


def side_by_side(ref, at):
    return jnp.concatenate([ref[at + i] for i in range(CHUNK)], axis=1)


def put_apart(ref, at, value):
    for i in range(CHUNK):
        ref[at + i] = value[:, i * WIDTH : (i + 1) * WIDTH]


def forward_kernel(
    spec, cot, courant, upwind, w_in, b_in, w_mid, b_mid, w_out_t, b_out,
    act_one, slope_one, act_two, slope_two, damped, driven, inside, sent,
    w_in_t, b_in_c, w_mid_t, b_mid_c, b_out_c,
):
    step = pl.program_id(0)

    @pl.when(step == 0)
    def _():
        set_weights(w_in, b_in, w_mid, b_mid, w_out_t, b_out, w_in_t, b_in_c, w_mid_t, b_mid_c, b_out_c)

    for part in range(BLOCK // CHUNK):
        at = part * CHUNK
        x = side_by_side(spec, at)
        _, a1, s1, a2, s2, damping, logistic = forward(
            x, w_in_t[...], b_in_c[...], w_mid_t[...], b_mid_c[...], w_out_t[...], b_out_c[...]
        )
        act_one[part] = a1
        slope_one[part] = s1
        act_two[part] = a2
        slope_two[part] = s2
        damped[part] = time_step * damping
        driven[part] = (-time_step) * x * logistic
        for i in range(CHUNK):
            d = step * BLOCK + at + i
            columns = slice(i * WIDTH, (i + 1) * WIDTH)
            up, c = upwind[pl.ds(d, 1), :], courant[pl.ds(d, 1), :]
            index = jnp.broadcast_to(up, (FREQS, WIDTH))
            own = spec[at + i]
            upstream = jnp.where(from_inside(index), gathered(own, index + HALO), 0.0)
            damp = time_step * damping[:, columns]
            inside[part, :, columns] = own - c * (own - upstream) - damp * own
            hot = one_hot(jnp.broadcast_to(up - HALO, (WIDTH, WIDTH)))
            sent[part, :, columns] = spread(c * cot[at + i], hot)


def weight_specs():
    fixed = lambda i: (0, 0)
    return [
        pl.BlockSpec((FREQS, HID), fixed),
        pl.BlockSpec((1, HID), fixed),
        pl.BlockSpec((HID, HID), fixed),
        pl.BlockSpec((1, HID), fixed),
        pl.BlockSpec((FREQS, HID), fixed),
        pl.BlockSpec((1, FREQS), fixed),
    ]


def weight_scratch():
    return [
        pltpu.VMEM((HID, FREQS), BF16),
        pltpu.VMEM((HID, HID), F32),
        pltpu.VMEM((HID, HID), BF16),
        pltpu.VMEM((HID, HID), F32),
        pltpu.VMEM((FREQS, HID), F32),
    ]


PARTS = DIRS // CHUNK
SPAN = CHUNK * WIDTH


def saved_specs():
    per = BLOCK // CHUNK
    hid = pl.BlockSpec((per, HID, SPAN), lambda i: (i, 0, 0))
    freq = pl.BlockSpec((per, FREQS, SPAN), lambda i: (i, 0, 0))
    return [hid, hid, hid, hid, freq, freq, freq, freq]


def directions(rows=FREQS):
    return pl.BlockSpec((BLOCK, rows, WIDTH), lambda i: (i, 0, 0))


def whole_rows():
    return pl.BlockSpec((DIRS, WIDTH), lambda i: (0, 0))


def forward_saved(field, cotangent, courant, upwind, weights):
    hid = lambda kind: jax.ShapeDtypeStruct((PARTS, HID, SPAN), kind)
    freq = jax.ShapeDtypeStruct((PARTS, FREQS, SPAN), F32)
    return pl.pallas_call(
        forward_kernel,
        grid=(DIRS // BLOCK,),
        in_specs=[directions(), directions(), whole_rows(), whole_rows()] + weight_specs(),
        out_specs=saved_specs(),
        out_shape=[hid(BF16), hid(F32), hid(BF16), hid(F32), freq, freq, freq, freq],
        scratch_shapes=weight_scratch(),
        compiler_params=pltpu.CompilerParams(vmem_limit_bytes=LIMIT),
        cost_estimate=pl.CostEstimate(
            flops=2 * 24576 * DIRS * WIDTH, bytes_accessed=9_000_000, transcendentals=2 * HID * DIRS * WIDTH
        ),
        name="forward_start",
    )(*in_hbm(field, cotangent, courant, upwind, *weights))


def adjoint(incoming, rounded, driven, a1, s1, a2, s2, w_in, w_mid, w_out, grads, b_out_sum):
    width = incoming.shape[1]
    ones = jnp.ones((16, width), BF16)
    g_source = (incoming * driven).astype(BF16)
    grads[160:192] += dot_nt(g_source, a2)
    b_out_sum[...] += sum(
        g_source[:, i * WIDTH : (i + 1) * WIDTH].astype(F32) for i in range(width // WIDTH)
    )
    back_two = (dot(w_out, g_source) * s2).astype(BF16)
    grad = dot_nt(jnp.concatenate([a1, ones], axis=0), back_two)
    grads[:128] += grad[:128]
    grads[193:194] += grad[128:129]
    back_one = (dot(w_mid, back_two) * s1).astype(BF16)
    grad = dot_nt(jnp.concatenate([rounded, ones], axis=0), back_one)
    grads[128:160] += grad[:32]
    grads[192:193] += grad[32:33]
    return dot(w_in, back_one)


def main_kernel(
    spec, cot, courant, upwind, far, near, far_tail, near_tail,
    act_one, slope_one, act_two, slope_two, damped, driven, inside, sent,
    w_in, b_in, w_mid, b_mid, w_out_t, b_out,
    middle_out, rest_out, grads,
    w_in_t, b_in_c, w_mid_t, b_mid_c, b_out_c, w_out, b_out_sum, rim_cs, rim_us,
):
    step = pl.program_id(0)

    @pl.when(step == 0)
    def _():
        set_weights(
            w_in, b_in, w_mid, b_mid, w_out_t, b_out, w_in_t, b_in_c, w_mid_t, b_mid_c, b_out_c, w_out
        )
        set_rim(far_tail, near_tail, rim_cs, rim_us)
        grads[...] = jnp.zeros_like(grads)
        b_out_sum[...] = jnp.zeros_like(b_out_sum)

    odd = is_odd()
    sides = (lanes((FREQS, WIDTH)) < HALO).astype(jnp.int32)
    far_side = jnp.where(odd, 1 - sides, sides) == 1
    for part in range(BLOCK // CHUNK):
        at = part * CHUNK
        outside, courants, from_rim = [], [], []
        for i in range(CHUNK):
            d = step * BLOCK + at + i
            rows = slice((at + i) * FREQS, (at + i + 1) * FREQS)
            rim_x = jnp.where(far_side, far[rows], near[rows])
            rim_g = jnp.where(far_side, near[rows], far[rows])
            index = jnp.broadcast_to(upwind[pl.ds(d, 1), :], (FREQS, WIDTH))
            c = jnp.broadcast_to(courant[pl.ds(d, 1), :], (FREQS, WIDTH))
            outside.append(jnp.where(from_inside(index), 0.0, c * gathered(rim_x, index)))
            courants.append(c)
            rim_c, rim_u = rim_cs[pl.ds(d, 1), :], rim_us[pl.ds(d, 1), :]
            from_rim.append(spread(rim_c * rim_g, one_hot(jnp.broadcast_to(rim_u, (WIDTH, WIDTH)))))
        x = side_by_side(spec, at)
        g = side_by_side(cot, at)
        c = jnp.concatenate(courants, axis=1)
        field = inside[part] + jnp.concatenate(outside, axis=1)
        rounded, a1, s1, a2, s2, damping, logistic = forward(
            field, w_in_t[...], b_in_c[...], w_mid_t[...], b_mid_c[...], w_out_t[...], b_out_c[...]
        )
        back = adjoint(
            g, rounded, (-time_step) * field * logistic, a1, s1, a2, s2,
            w_in[...], w_mid[...], w_out[...], grads, b_out_sum,
        )
        middle = (
            g * (1.0 - c - time_step * damping) + back + sent[part] + jnp.concatenate(from_rim, axis=1)
        )
        back = adjoint(
            middle, x.astype(BF16), driven[part], act_one[part], slope_one[part], act_two[part],
            slope_two[part], w_in[...], w_mid[...], w_out[...], grads, b_out_sum,
        )
        put_apart(middle_out, at, middle)
        put_apart(rest_out, at, middle * (1.0 - c - damped[part]) + back)

    @pl.when(step == pl.num_programs(0) - 1)
    def _():
        grads[194:195, :FREQS] = jnp.sum(b_out_sum[...].T, axis=0, keepdims=True)


def both_adjoints(field, cotangent, courant, upwind, far, near, saved, weights):
    halo = pl.BlockSpec((BLOCK * FREQS, WIDTH), lambda i: (i, 0))
    tail = pl.BlockSpec((TAIL, WIDTH), lambda i: (DIRS * FREQS // TAIL, 0))
    state = jax.ShapeDtypeStruct((DIRS, FREQS, WIDTH), F32)
    return pl.pallas_call(
        main_kernel,
        grid=(DIRS // BLOCK,),
        in_specs=[directions(), directions(), whole_rows(), whole_rows(), halo, halo, tail, tail]
        + saved_specs()
        + weight_specs(),
        out_specs=[directions(), directions(), pl.BlockSpec((ROWS, WIDTH), lambda i: (0, 0))],
        out_shape=[state, state, jax.ShapeDtypeStruct((ROWS, WIDTH), F32)],
        scratch_shapes=weight_scratch()
        + [
            pltpu.VMEM((HID, FREQS), BF16),
            pltpu.VMEM((FREQS, WIDTH), F32),
            pltpu.VMEM((TAIL, WIDTH), F32),
            pltpu.VMEM((TAIL, WIDTH), jnp.int32),
        ],
        compiler_params=pltpu.CompilerParams(vmem_limit_bytes=LIMIT),
        cost_estimate=pl.CostEstimate(
            flops=10 * 24576 * DIRS * WIDTH, bytes_accessed=14_000_000, transcendentals=2 * HID * DIRS * WIDTH
        ),
        name="both_adjoints",
    )(field, cotangent, courant, upwind, far, near, far, near, *saved, *weights)


def edge_kernel(middle, to_far, to_near):
    odd = is_odd()
    first, second = middle[:, : FREQS // 2, :], middle[:, FREQS // 2 :, :]
    to_next = low_lanes(turned(first), second)
    to_prev = low_lanes(first, turned(second))
    to_far[...] = jnp.where(odd, to_next, to_prev)
    to_near[...] = jnp.where(odd, to_prev, to_next)


def packed_edges(middle):
    half = jax.ShapeDtypeStruct((DIRS, FREQS // 2, WIDTH), F32)
    return pl.pallas_call(
        edge_kernel,
        out_shape=(half, half),
        compiler_params=pltpu.CompilerParams(vmem_limit_bytes=LIMIT),
        cost_estimate=pl.CostEstimate(flops=1_000_000, bytes_accessed=1_200_000, transcendentals=0),
        name="pack_edges",
    )(middle)


def last_kernel(rest, middle, courant, upwind, far, near, far_tail, near_tail, out, rim_cs, rim_us):
    step = pl.program_id(0)

    @pl.when(step == 0)
    def _():
        set_rim(far_tail, near_tail, rim_cs, rim_us)

    odd = is_odd()
    for i in range(BLOCK):
        d = step * BLOCK + i
        low, high = jnp.where(odd, near[i], far[i]), jnp.where(odd, far[i], near[i])
        rim = jnp.concatenate([low_lanes(high, turned(low)), low_lanes(turned(high), low)], axis=0)
        rim_c, rim_u = rim_cs[pl.ds(d, 1), :], rim_us[pl.ds(d, 1), :]
        own_u = upwind[pl.ds(d, 1), :] - HALO
        hot = jnp.concatenate(
            [one_hot(jnp.broadcast_to(u, (WIDTH, WIDTH))) for u in (own_u, rim_u)], axis=1
        )
        moved = jnp.concatenate([courant[pl.ds(d, 1), :] * middle[i], rim_c * rim], axis=1)
        out[0, i] = rest[i] + spread(moved, hot)


def last_state(rest, middle, courant, upwind, far, near, far_first, near_first):
    tail = pl.BlockSpec((TAIL, WIDTH), lambda i: (DIRS * FREQS // TAIL, 0))
    edges = directions(FREQS // 2)
    return pl.pallas_call(
        last_kernel,
        grid=(DIRS // BLOCK,),
        in_specs=[directions(), directions(), whole_rows(), whole_rows(), edges, edges, tail, tail],
        out_specs=pl.BlockSpec((1, BLOCK, FREQS, WIDTH), lambda i: (0, i, 0, 0)),
        out_shape=jax.ShapeDtypeStruct((1, DIRS, FREQS, WIDTH), F32),
        scratch_shapes=[pltpu.VMEM((TAIL, WIDTH), F32), pltpu.VMEM((TAIL, WIDTH), jnp.int32)],
        compiler_params=pltpu.CompilerParams(vmem_limit_bytes=LIMIT),
        cost_estimate=pl.CostEstimate(
            flops=8 * FREQS * WIDTH * WIDTH * DIRS, bytes_accessed=2_400_000, transcendentals=0
        ),
        name="last_state",
    )(rest, middle, courant, upwind, far, near, far_first, near_first)


def clip_kernel(whole, w_in, b_in, w_mid, b_mid, w_out_t, b_out):
    x = whole[...]
    squares = jnp.sum(x * x, keepdims=True)
    factor = clip_norm / jnp.maximum(jnp.sqrt(squares), clip_norm)
    w_mid[...] = x[:128] * factor
    w_in[...] = x[128:160] * factor
    w_out_t[...] = x[160:192] * factor
    b_in[...] = x[192:193] * factor
    b_mid[...] = x[193:194] * factor
    b_out[...] = x[194:195, :FREQS] * factor


def clipped(whole):
    shape = lambda *s: jax.ShapeDtypeStruct(s, F32)
    w_in, b_in, w_mid, b_mid, w_out_t, b_out = pl.pallas_call(
        clip_kernel,
        out_shape=[
            shape(FREQS, HID),
            shape(1, HID),
            shape(HID, HID),
            shape(1, HID),
            shape(FREQS, HID),
            shape(1, FREQS),
        ],
        compiler_params=pltpu.CompilerParams(vmem_limit_bytes=LIMIT),
        name="clip",
    )(whole)
    return (w_in, b_in[0], w_mid, b_mid[0], w_out_t.T, b_out[0])


def exchanged(blocks, groups):
    return lax.all_to_all(
        blocks, ("space", "case"), 0, 0, axis_index_groups=groups, tiled=True
    )


def copied(parts, copies):
    total = jnp.sum(parts, axis=0)
    return jnp.broadcast_to(total[None], (copies,) + total.shape)


def device_groups():
    spaces, cases = lax.axis_size("space"), lax.axis_size("case")
    grid = np.arange(spaces * cases).reshape(spaces // 32, 4, 8, cases)
    along = lambda axis: np.moveaxis(grid, axis, -1).reshape(-1, grid.shape[axis]).tolist()
    return [along(axis) for axis in range(4)]


def summed_everywhere(parts):
    z_lo, x, y_core, z_hi = device_groups()
    first, second = len(y_core[0]), len(x[0])
    rows = ROWS // first
    parts = exchanged(parts.reshape(first, rows, WIDTH), y_core)
    parts = exchanged(jnp.sum(parts, axis=0).reshape(second, rows // second, WIDTH), x)
    parts = exchanged(copied(parts, len(z_lo[0])), z_lo)
    parts = exchanged(copied(parts, len(z_hi[0])), z_hi)
    parts = exchanged(copied(parts, second), x)
    whole = jnp.broadcast_to(parts.reshape(1, rows, WIDTH), (first, rows, WIDTH))
    return exchanged(whole, y_core).reshape(ROWS, WIDTH)


def by_pairs(far, near):
    count = lax.axis_size("space")
    swapped = lambda first: [
        pair for i in range(first, count - 1, 2) for pair in ((i, i + 1), (i + 1, i))
    ]
    return lax.ppermute(far, "space", swapped(1)), lax.ppermute(near, "space", swapped(0))


def shards(spectrum, cotangent, courant, upwind, w_in, b_in, w_mid, b_mid, w_out, b_out):
    weights = (w_in, b_in[None], w_mid, b_mid[None], w_out.T, b_out[None])
    field, incoming = spectrum[0], cotangent[0]
    far, near = by_pairs(*packed_halo(spectrum, cotangent, courant, upwind))
    saved = forward_saved(field, incoming, courant, upwind, weights)
    middle, rest, grads = both_adjoints(
        field, incoming, courant, upwind, far, near, saved, weights
    )
    totals = clipped(summed_everywhere(grads))
    far_mid, near_mid = by_pairs(*packed_edges(middle))
    state = last_state(rest, middle, courant, upwind, far_mid, near_mid, far, near)
    return (state, *totals)


def solution(mesh):
    placed = (
        P("case", None, None, "space"),
        P("case", None, None, "space"),
        P(None, "space"),
        P(None, "space"),
        P(),
        P(),
        P(),
        P(),
        P(),
        P(),
    )
    return jax.shard_map(
        shards,
        mesh=mesh,
        in_specs=placed,
        out_specs=(P("case", None, None, "space"), P(), P(), P(), P(), P(), P()),
        check_vma=False,
    )
```

```python
import jax
import jax.numpy as jnp
import numpy as np
from jax import lax
from jax.experimental import pallas as pl
from jax.experimental.pallas import tpu as pltpu
from jax.sharding import PartitionSpec as P

DIRS = 36
FREQS = 32
HID = 128
HALO = 64
WIDTH = 128
TAIL = 48
CHUNK = 12
BLOCK = 12
ROWS = 256

time_step = 0.3
clip_norm = 100.0
F32 = jnp.float32
BF16 = jnp.bfloat16
LIMIT = 40 * 1024 * 1024


def dot(a, b):
    return jnp.dot(a, b, preferred_element_type=F32)


def dot_nt(a, b):
    return lax.dot_general(a, b, (((1,), (1,)), ((), ())), preferred_element_type=F32)


def lanes(shape):
    return lax.broadcasted_iota(jnp.int32, shape, len(shape) - 1)


def turned(x):
    return pltpu.roll(x, HALO, x.ndim - 1)


def low_lanes(a, b):
    return jnp.where(lanes(a.shape) < HALO, a, b)


def in_hbm(*arrays):
    return [pltpu.with_memory_space_constraint(x, pltpu.HBM) for x in arrays]


def is_odd():
    return lax.axis_index("space") % 2 == 1


def pack_kernel(spec, cot, courant, upwind, far, near):
    main = DIRS * FREQS
    sides = lanes((8, WIDTH)) < HALO
    mine = jnp.where(is_odd(), sides.astype(jnp.int32), 1 - sides.astype(jnp.int32))

    def put(rows, x, g):
        here = jnp.broadcast_to(mine[:1], x.shape) == 1
        x = turned(x)
        far[rows] = jnp.where(here, x, g)
        near[rows] = jnp.where(here, g, x)

    put(slice(0, main), spec[0].reshape(main, WIDTH), cot[0].reshape(main, WIDTH))
    put(slice(main, main + DIRS), upwind[...].astype(F32), courant[...])
    rest = jnp.zeros((TAIL - DIRS, WIDTH), F32)
    far[main + DIRS :] = rest
    near[main + DIRS :] = rest


def packed_halo(spectrum, cotangent, courant, upwind):
    out = jax.ShapeDtypeStruct((DIRS * FREQS + TAIL, WIDTH), F32)
    return pl.pallas_call(
        pack_kernel,
        out_shape=(out, out),
        compiler_params=pltpu.CompilerParams(vmem_limit_bytes=LIMIT),
        name="pack_halo",
    )(*in_hbm(spectrum, cotangent, courant, upwind))


def set_rim(far, near, rim_c, rim_u):
    odd = is_odd()
    below = jnp.where(odd, near[...], far[...])
    above = jnp.where(odd, far[...], near[...])
    rim_c[...] = low_lanes(above, below)
    own = turned(low_lanes(below, above))
    offset = jnp.where(lanes(own.shape) < HALO, WIDTH - HALO, -(HALO + WIDTH))
    rim_u[...] = own.astype(jnp.int32) + offset


def one_hot(target):
    place = lax.broadcasted_iota(jnp.int32, (WIDTH, WIDTH), 0)
    return jnp.where(place == target, 1.0, 0.0).astype(BF16)


def spread(value, hot):
    high = value.astype(BF16)
    low = (value - high.astype(F32)).astype(BF16)
    both = dot_nt(jnp.concatenate([high, low], axis=0), hot)
    return both[:FREQS] + both[FREQS:]


def gathered(x, index):
    return jnp.take_along_axis(x, index & (WIDTH - 1), axis=1, mode="promise_in_bounds")


def from_inside(index):
    return (index >= HALO) & (index < HALO + WIDTH)


def column(row):
    return jnp.broadcast_to(row, (HID, HID)).T


def wide(tile, width):
    return jnp.concatenate([tile] * (width // tile.shape[1]), axis=1)


def activated(pre):
    logistic = 0.5 + 0.5 * jnp.tanh(0.5 * pre)
    act = pre * logistic
    return act.astype(BF16), logistic + act * (1.0 - logistic)


def forward(x, w_in_t, b_in, w_mid_t, b_mid, w_out_t, b_out):
    width = x.shape[1]
    rounded = x.astype(BF16)
    act_one, slope_one = activated(dot(w_in_t, rounded) + wide(b_in, width))
    act_two, slope_two = activated(dot(w_mid_t, act_one) + wide(b_mid, width))
    source = dot(w_out_t, act_two) + wide(b_out, width)
    damping = jnp.maximum(source, 0.0) + jnp.log(1.0 + jnp.exp(-jnp.abs(source)))
    logistic = 0.5 + 0.5 * jnp.tanh(0.5 * source)
    return rounded, act_one, slope_one, act_two, slope_two, damping, logistic


def set_weights(w_in, b_in, w_mid, b_mid, w_out_t, b_out, w_in_t, b_in_c, w_mid_t, b_mid_c, b_out_c, w_out=None):
    w_in_t[...] = w_in[...].astype(F32).T.astype(BF16)
    w_mid_t[...] = w_mid[...].astype(F32).T.astype(BF16)
    b_in_c[...] = column(b_in[...])
    b_mid_c[...] = column(b_mid[...])
    row = jnp.broadcast_to(b_out[...], (HID, FREQS))
    b_out_c[...] = row.T
    if w_out is not None:
        w_out[...] = w_out_t[...].astype(F32).T.astype(BF16)


def side_by_side(ref, at):
    return jnp.concatenate([ref[at + i] for i in range(CHUNK)], axis=1)


def put_apart(ref, at, value):
    for i in range(CHUNK):
        ref[at + i] = value[:, i * WIDTH : (i + 1) * WIDTH]


def forward_kernel(
    spec, cot, courant, upwind, w_in, b_in, w_mid, b_mid, w_out_t, b_out,
    act_one, slope_one, act_two, slope_two, damped, driven, inside, sent,
    w_in_t, b_in_c, w_mid_t, b_mid_c, b_out_c,
):
    step = pl.program_id(0)

    @pl.when(step == 0)
    def _():
        set_weights(w_in, b_in, w_mid, b_mid, w_out_t, b_out, w_in_t, b_in_c, w_mid_t, b_mid_c, b_out_c)

    for part in range(BLOCK // CHUNK):
        at = part * CHUNK
        x = side_by_side(spec, at)
        _, a1, s1, a2, s2, damping, logistic = forward(
            x, w_in_t[...], b_in_c[...], w_mid_t[...], b_mid_c[...], w_out_t[...], b_out_c[...]
        )
        act_one[part] = a1
        slope_one[part] = s1
        act_two[part] = a2
        slope_two[part] = s2
        damped[part] = time_step * damping
        driven[part] = (-time_step) * x * logistic
        for i in range(CHUNK):
            d = step * BLOCK + at + i
            columns = slice(i * WIDTH, (i + 1) * WIDTH)
            up, c = upwind[pl.ds(d, 1), :], courant[pl.ds(d, 1), :]
            index = jnp.broadcast_to(up, (FREQS, WIDTH))
            own = spec[at + i]
            upstream = jnp.where(from_inside(index), gathered(own, index + HALO), 0.0)
            damp = time_step * damping[:, columns]
            inside[part, :, columns] = own - c * (own - upstream) - damp * own
            hot = one_hot(jnp.broadcast_to(up - HALO, (WIDTH, WIDTH)))
            sent[part, :, columns] = spread(c * cot[at + i], hot)


def weight_specs():
    fixed = lambda i: (0, 0)
    return [
        pl.BlockSpec((FREQS, HID), fixed),
        pl.BlockSpec((1, HID), fixed),
        pl.BlockSpec((HID, HID), fixed),
        pl.BlockSpec((1, HID), fixed),
        pl.BlockSpec((FREQS, HID), fixed),
        pl.BlockSpec((1, FREQS), fixed),
    ]


def weight_scratch():
    return [
        pltpu.VMEM((HID, FREQS), BF16),
        pltpu.VMEM((HID, HID), F32),
        pltpu.VMEM((HID, HID), BF16),
        pltpu.VMEM((HID, HID), F32),
        pltpu.VMEM((FREQS, HID), F32),
    ]


PARTS = DIRS // CHUNK
SPAN = CHUNK * WIDTH


def saved_specs():
    per = BLOCK // CHUNK
    hid = pl.BlockSpec((per, HID, SPAN), lambda i: (i, 0, 0))
    freq = pl.BlockSpec((per, FREQS, SPAN), lambda i: (i, 0, 0))
    return [hid, hid, hid, hid, freq, freq, freq, freq]


def directions(rows=FREQS):
    return pl.BlockSpec((BLOCK, rows, WIDTH), lambda i: (i, 0, 0))


def whole_rows():
    return pl.BlockSpec((DIRS, WIDTH), lambda i: (0, 0))


def forward_saved(field, cotangent, courant, upwind, weights):
    hid = lambda kind: jax.ShapeDtypeStruct((PARTS, HID, SPAN), kind)
    freq = jax.ShapeDtypeStruct((PARTS, FREQS, SPAN), F32)
    return pl.pallas_call(
        forward_kernel,
        grid=(DIRS // BLOCK,),
        in_specs=[directions(), directions(), whole_rows(), whole_rows()] + weight_specs(),
        out_specs=saved_specs(),
        out_shape=[hid(BF16), hid(F32), hid(BF16), hid(F32), freq, freq, freq, freq],
        scratch_shapes=weight_scratch(),
        compiler_params=pltpu.CompilerParams(vmem_limit_bytes=LIMIT),
        cost_estimate=pl.CostEstimate(
            flops=2 * 24576 * DIRS * WIDTH, bytes_accessed=9_000_000, transcendentals=2 * HID * DIRS * WIDTH
        ),
        name="forward_start",
    )(*in_hbm(field, cotangent, courant, upwind, *weights))


def adjoint(incoming, rounded, driven, a1, s1, a2, s2, w_in, w_mid, w_out, grads, b_out_sum):
    width = incoming.shape[1]
    ones = jnp.ones((16, width), BF16)
    g_source = (incoming * driven).astype(BF16)
    grads[160:192] += dot_nt(g_source, a2)
    b_out_sum[...] += sum(
        g_source[:, i * WIDTH : (i + 1) * WIDTH].astype(F32) for i in range(width // WIDTH)
    )
    back_two = (dot(w_out, g_source) * s2).astype(BF16)
    grad = dot_nt(jnp.concatenate([a1, ones], axis=0), back_two)
    grads[:128] += grad[:128]
    grads[193:194] += grad[128:129]
    back_one = (dot(w_mid, back_two) * s1).astype(BF16)
    grad = dot_nt(jnp.concatenate([rounded, ones], axis=0), back_one)
    grads[128:160] += grad[:32]
    grads[192:193] += grad[32:33]
    return dot(w_in, back_one)


def main_kernel(
    spec, cot, courant, upwind, far, near, far_tail, near_tail,
    act_one, slope_one, act_two, slope_two, damped, driven, inside, sent,
    w_in, b_in, w_mid, b_mid, w_out_t, b_out,
    middle_out, rest_out, grads,
    w_in_t, b_in_c, w_mid_t, b_mid_c, b_out_c, w_out, b_out_sum, rim_cs, rim_us,
):
    step = pl.program_id(0)

    @pl.when(step == 0)
    def _():
        set_weights(
            w_in, b_in, w_mid, b_mid, w_out_t, b_out, w_in_t, b_in_c, w_mid_t, b_mid_c, b_out_c, w_out
        )
        set_rim(far_tail, near_tail, rim_cs, rim_us)
        grads[...] = jnp.zeros_like(grads)
        b_out_sum[...] = jnp.zeros_like(b_out_sum)

    odd = is_odd()
    sides = (lanes((FREQS, WIDTH)) < HALO).astype(jnp.int32)
    far_side = jnp.where(odd, 1 - sides, sides) == 1
    for part in range(BLOCK // CHUNK):
        at = part * CHUNK
        outside, courants, from_rim = [], [], []
        for i in range(CHUNK):
            d = step * BLOCK + at + i
            rows = slice((at + i) * FREQS, (at + i + 1) * FREQS)
            rim_x = jnp.where(far_side, far[rows], near[rows])
            rim_g = jnp.where(far_side, near[rows], far[rows])
            index = jnp.broadcast_to(upwind[pl.ds(d, 1), :], (FREQS, WIDTH))
            c = jnp.broadcast_to(courant[pl.ds(d, 1), :], (FREQS, WIDTH))
            outside.append(jnp.where(from_inside(index), 0.0, c * gathered(rim_x, index)))
            courants.append(c)
            rim_c, rim_u = rim_cs[pl.ds(d, 1), :], rim_us[pl.ds(d, 1), :]
            from_rim.append(spread(rim_c * rim_g, one_hot(jnp.broadcast_to(rim_u, (WIDTH, WIDTH)))))
        x = side_by_side(spec, at)
        g = side_by_side(cot, at)
        c = jnp.concatenate(courants, axis=1)
        field = inside[part] + jnp.concatenate(outside, axis=1)
        rounded, a1, s1, a2, s2, damping, logistic = forward(
            field, w_in_t[...], b_in_c[...], w_mid_t[...], b_mid_c[...], w_out_t[...], b_out_c[...]
        )
        back = adjoint(
            g, rounded, (-time_step) * field * logistic, a1, s1, a2, s2,
            w_in[...], w_mid[...], w_out[...], grads, b_out_sum,
        )
        middle = (
            g * (1.0 - c - time_step * damping) + back + sent[part] + jnp.concatenate(from_rim, axis=1)
        )
        back = adjoint(
            middle, x.astype(BF16), driven[part], act_one[part], slope_one[part], act_two[part],
            slope_two[part], w_in[...], w_mid[...], w_out[...], grads, b_out_sum,
        )
        put_apart(middle_out, at, middle)
        put_apart(rest_out, at, middle * (1.0 - c - damped[part]) + back)

    @pl.when(step == pl.num_programs(0) - 1)
    def _():
        grads[194:195, :FREQS] = jnp.sum(b_out_sum[...].T, axis=0, keepdims=True)


def both_adjoints(field, cotangent, courant, upwind, far, near, saved, weights):
    halo = pl.BlockSpec((BLOCK * FREQS, WIDTH), lambda i: (i, 0))
    tail = pl.BlockSpec((TAIL, WIDTH), lambda i: (DIRS * FREQS // TAIL, 0))
    state = jax.ShapeDtypeStruct((DIRS, FREQS, WIDTH), F32)
    return pl.pallas_call(
        main_kernel,
        grid=(DIRS // BLOCK,),
        in_specs=[directions(), directions(), whole_rows(), whole_rows(), halo, halo, tail, tail]
        + saved_specs()
        + weight_specs(),
        out_specs=[directions(), directions(), pl.BlockSpec((ROWS, WIDTH), lambda i: (0, 0))],
        out_shape=[state, state, jax.ShapeDtypeStruct((ROWS, WIDTH), F32)],
        scratch_shapes=weight_scratch()
        + [
            pltpu.VMEM((HID, FREQS), BF16),
            pltpu.VMEM((FREQS, WIDTH), F32),
            pltpu.VMEM((TAIL, WIDTH), F32),
            pltpu.VMEM((TAIL, WIDTH), jnp.int32),
        ],
        compiler_params=pltpu.CompilerParams(vmem_limit_bytes=LIMIT),
        cost_estimate=pl.CostEstimate(
            flops=10 * 24576 * DIRS * WIDTH, bytes_accessed=14_000_000, transcendentals=2 * HID * DIRS * WIDTH
        ),
        name="both_adjoints",
    )(field, cotangent, courant, upwind, far, near, far, near, *saved, *weights)


def edge_kernel(middle, to_far, to_near):
    odd = is_odd()
    first, second = middle[:, : FREQS // 2, :], middle[:, FREQS // 2 :, :]
    to_next = low_lanes(turned(first), second)
    to_prev = low_lanes(first, turned(second))
    to_far[...] = jnp.where(odd, to_next, to_prev)
    to_near[...] = jnp.where(odd, to_prev, to_next)


def packed_edges(middle):
    half = jax.ShapeDtypeStruct((DIRS, FREQS // 2, WIDTH), F32)
    return pl.pallas_call(
        edge_kernel,
        out_shape=(half, half),
        compiler_params=pltpu.CompilerParams(vmem_limit_bytes=LIMIT),
        cost_estimate=pl.CostEstimate(flops=1_000_000, bytes_accessed=1_200_000, transcendentals=0),
        name="pack_edges",
    )(middle)


def last_kernel(rest, middle, courant, upwind, far, near, far_tail, near_tail, out, rim_cs, rim_us):
    step = pl.program_id(0)

    @pl.when(step == 0)
    def _():
        set_rim(far_tail, near_tail, rim_cs, rim_us)

    odd = is_odd()
    for i in range(BLOCK):
        d = step * BLOCK + i
        low, high = jnp.where(odd, near[i], far[i]), jnp.where(odd, far[i], near[i])
        rim = jnp.concatenate([low_lanes(high, turned(low)), low_lanes(turned(high), low)], axis=0)
        rim_c, rim_u = rim_cs[pl.ds(d, 1), :], rim_us[pl.ds(d, 1), :]
        own_u = upwind[pl.ds(d, 1), :] - HALO
        hot = jnp.concatenate(
            [one_hot(jnp.broadcast_to(u, (WIDTH, WIDTH))) for u in (own_u, rim_u)], axis=1
        )
        moved = jnp.concatenate([courant[pl.ds(d, 1), :] * middle[i], rim_c * rim], axis=1)
        out[0, i] = rest[i] + spread(moved, hot)


def last_state(rest, middle, courant, upwind, far, near, far_first, near_first):
    tail = pl.BlockSpec((TAIL, WIDTH), lambda i: (DIRS * FREQS // TAIL, 0))
    edges = directions(FREQS // 2)
    return pl.pallas_call(
        last_kernel,
        grid=(DIRS // BLOCK,),
        in_specs=[directions(), directions(), whole_rows(), whole_rows(), edges, edges, tail, tail],
        out_specs=pl.BlockSpec((1, BLOCK, FREQS, WIDTH), lambda i: (0, i, 0, 0)),
        out_shape=jax.ShapeDtypeStruct((1, DIRS, FREQS, WIDTH), F32),
        scratch_shapes=[pltpu.VMEM((TAIL, WIDTH), F32), pltpu.VMEM((TAIL, WIDTH), jnp.int32)],
        compiler_params=pltpu.CompilerParams(vmem_limit_bytes=LIMIT),
        cost_estimate=pl.CostEstimate(
            flops=8 * FREQS * WIDTH * WIDTH * DIRS, bytes_accessed=2_400_000, transcendentals=0
        ),
        name="last_state",
    )(rest, middle, courant, upwind, far, near, far_first, near_first)


def clip_kernel(whole, w_in, b_in, w_mid, b_mid, w_out_t, b_out):
    x = whole[...]
    squares = jnp.sum(x * x, keepdims=True)
    factor = clip_norm / jnp.maximum(jnp.sqrt(squares), clip_norm)
    w_mid[...] = x[:128] * factor
    w_in[...] = x[128:160] * factor
    w_out_t[...] = x[160:192] * factor
    b_in[...] = x[192:193] * factor
    b_mid[...] = x[193:194] * factor
    b_out[...] = x[194:195, :FREQS] * factor


def clipped(whole):
    shape = lambda *s: jax.ShapeDtypeStruct(s, F32)
    w_in, b_in, w_mid, b_mid, w_out_t, b_out = pl.pallas_call(
        clip_kernel,
        out_shape=[
            shape(FREQS, HID),
            shape(1, HID),
            shape(HID, HID),
            shape(1, HID),
            shape(FREQS, HID),
            shape(1, FREQS),
        ],
        compiler_params=pltpu.CompilerParams(vmem_limit_bytes=LIMIT),
        name="clip",
    )(whole)
    return (w_in, b_in[0], w_mid, b_mid[0], w_out_t.T, b_out[0])


def exchanged(blocks, groups):
    return lax.all_to_all(
        blocks, ("space", "case"), 0, 0, axis_index_groups=groups, tiled=True
    )


def copied(parts, copies):
    total = jnp.sum(parts, axis=0)
    return jnp.broadcast_to(total[None], (copies,) + total.shape)


def device_groups():
    spaces, cases = lax.axis_size("space"), lax.axis_size("case")
    grid = np.arange(spaces * cases).reshape(spaces // 32, 32, cases)
    layers = grid.transpose(0, 2, 1).reshape(-1, 32)
    columns = grid.transpose(1, 0, 2).reshape(32, -1)
    return layers.tolist(), columns.tolist()


def summed_everywhere(parts):
    layers, columns = device_groups()
    wide, deep = len(layers[0]), len(columns[0])
    parts = exchanged(parts.reshape(wide, ROWS // wide, WIDTH), layers)
    parts = exchanged(copied(parts, deep), columns)
    return exchanged(copied(parts, wide), layers).reshape(ROWS, WIDTH)


def by_pairs(far, near):
    count = lax.axis_size("space")
    swapped = lambda first: [
        pair for i in range(first, count - 1, 2) for pair in ((i, i + 1), (i + 1, i))
    ]
    return lax.ppermute(far, "space", swapped(1)), lax.ppermute(near, "space", swapped(0))


def shards(spectrum, cotangent, courant, upwind, w_in, b_in, w_mid, b_mid, w_out, b_out):
    weights = (w_in, b_in[None], w_mid, b_mid[None], w_out.T, b_out[None])
    field, incoming = spectrum[0], cotangent[0]
    far, near = by_pairs(*packed_halo(spectrum, cotangent, courant, upwind))
    saved = forward_saved(field, incoming, courant, upwind, weights)
    middle, rest, grads = both_adjoints(
        field, incoming, courant, upwind, far, near, saved, weights
    )
    totals = clipped(summed_everywhere(grads))
    far_mid, near_mid = by_pairs(*packed_edges(middle))
    state = last_state(rest, middle, courant, upwind, far_mid, near_mid, far, near)
    return (state, *totals)


def solution(mesh):
    placed = (
        P("case", None, None, "space"),
        P("case", None, None, "space"),
        P(None, "space"),
        P(None, "space"),
        P(),
        P(),
        P(),
        P(),
        P(),
        P(),
    )
    return jax.shard_map(
        shards,
        mesh=mesh,
        in_specs=placed,
        out_specs=(P("case", None, None, "space"), P(), P(), P(), P(), P(), P()),
        check_vma=False,
    )
```

```python
import jax
import jax.numpy as jnp
import numpy as np
from jax import lax
from jax.experimental import pallas as pl
from jax.experimental.pallas import tpu as pltpu
from jax.sharding import PartitionSpec as P

DIRS = 36
FREQS = 32
HID = 128
HALO = 64
WIDTH = 128
TAIL = 48
CHUNK = 12
BLOCK = 12
ROWS = 256

time_step = 0.3
clip_norm = 100.0
F32 = jnp.float32
BF16 = jnp.bfloat16
LIMIT = 40 * 1024 * 1024


def dot(a, b):
    return jnp.dot(a, b, preferred_element_type=F32)


def dot_nt(a, b):
    return lax.dot_general(a, b, (((1,), (1,)), ((), ())), preferred_element_type=F32)


def lanes(shape):
    return lax.broadcasted_iota(jnp.int32, shape, len(shape) - 1)


def turned(x):
    return pltpu.roll(x, HALO, x.ndim - 1)


def low_lanes(a, b):
    return jnp.where(lanes(a.shape) < HALO, a, b)


def in_hbm(*arrays):
    return [pltpu.with_memory_space_constraint(x, pltpu.HBM) for x in arrays]


def is_odd():
    return lax.axis_index("space") % 2 == 1


def pack_kernel(spec, cot, courant, upwind, far, near):
    main = DIRS * FREQS
    sides = lanes((8, WIDTH)) < HALO
    mine = jnp.where(is_odd(), sides.astype(jnp.int32), 1 - sides.astype(jnp.int32))

    def put(rows, x, g):
        here = jnp.broadcast_to(mine[:1], x.shape) == 1
        x = turned(x)
        far[rows] = jnp.where(here, x, g)
        near[rows] = jnp.where(here, g, x)

    put(slice(0, main), spec[0].reshape(main, WIDTH), cot[0].reshape(main, WIDTH))
    put(slice(main, main + DIRS), upwind[...].astype(F32), courant[...])
    rest = jnp.zeros((TAIL - DIRS, WIDTH), F32)
    far[main + DIRS :] = rest
    near[main + DIRS :] = rest


def packed_halo(spectrum, cotangent, courant, upwind):
    out = jax.ShapeDtypeStruct((DIRS * FREQS + TAIL, WIDTH), F32)
    return pl.pallas_call(
        pack_kernel,
        out_shape=(out, out),
        compiler_params=pltpu.CompilerParams(vmem_limit_bytes=LIMIT),
        name="pack_halo",
    )(*in_hbm(spectrum, cotangent, courant, upwind))


def set_rim(far, near, rim_c, rim_u):
    odd = is_odd()
    below = jnp.where(odd, near[...], far[...])
    above = jnp.where(odd, far[...], near[...])
    rim_c[...] = low_lanes(above, below)
    own = turned(low_lanes(below, above))
    offset = jnp.where(lanes(own.shape) < HALO, WIDTH - HALO, -(HALO + WIDTH))
    rim_u[...] = own.astype(jnp.int32) + offset


def one_hot(target):
    place = lax.broadcasted_iota(jnp.int32, (WIDTH, WIDTH), 0)
    return jnp.where(place == target, 1.0, 0.0).astype(BF16)


def spread(value, hot):
    high = value.astype(BF16)
    low = (value - high.astype(F32)).astype(BF16)
    both = dot_nt(jnp.concatenate([high, low], axis=0), hot)
    return both[:FREQS] + both[FREQS:]


def gathered(x, index):
    return jnp.take_along_axis(x, index & (WIDTH - 1), axis=1, mode="promise_in_bounds")


def from_inside(index):
    return (index >= HALO) & (index < HALO + WIDTH)


def column(row):
    return jnp.broadcast_to(row, (HID, HID)).T


def wide(tile, width):
    return jnp.concatenate([tile] * (width // tile.shape[1]), axis=1)


def activated(pre):
    logistic = 0.5 + 0.5 * jnp.tanh(0.5 * pre)
    act = pre * logistic
    return act.astype(BF16), logistic + act * (1.0 - logistic)


def forward(x, w_in_t, b_in, w_mid_t, b_mid, w_out_t, b_out):
    width = x.shape[1]
    rounded = x.astype(BF16)
    act_one, slope_one = activated(dot(w_in_t, rounded) + wide(b_in, width))
    act_two, slope_two = activated(dot(w_mid_t, act_one) + wide(b_mid, width))
    source = dot(w_out_t, act_two) + wide(b_out, width)
    damping = jnp.maximum(source, 0.0) + jnp.log(1.0 + jnp.exp(-jnp.abs(source)))
    logistic = 0.5 + 0.5 * jnp.tanh(0.5 * source)
    return rounded, act_one, slope_one, act_two, slope_two, damping, logistic


def set_weights(w_in, b_in, w_mid, b_mid, w_out_t, b_out, w_in_t, b_in_c, w_mid_t, b_mid_c, b_out_c, w_out=None):
    w_in_t[...] = w_in[...].astype(F32).T.astype(BF16)
    w_mid_t[...] = w_mid[...].astype(F32).T.astype(BF16)
    b_in_c[...] = column(b_in[...])
    b_mid_c[...] = column(b_mid[...])
    row = jnp.broadcast_to(b_out[...], (HID, FREQS))
    b_out_c[...] = row.T
    if w_out is not None:
        w_out[...] = w_out_t[...].astype(F32).T.astype(BF16)


def side_by_side(ref, at):
    return jnp.concatenate([ref[at + i] for i in range(CHUNK)], axis=1)


def put_apart(ref, at, value):
    for i in range(CHUNK):
        ref[at + i] = value[:, i * WIDTH : (i + 1) * WIDTH]


def forward_kernel(
    spec, cot, courant, upwind, w_in, b_in, w_mid, b_mid, w_out_t, b_out,
    act_one, slope_one, act_two, slope_two, damped, driven, inside, sent,
    w_in_t, b_in_c, w_mid_t, b_mid_c, b_out_c,
):
    step = pl.program_id(0)

    @pl.when(step == 0)
    def _():
        set_weights(w_in, b_in, w_mid, b_mid, w_out_t, b_out, w_in_t, b_in_c, w_mid_t, b_mid_c, b_out_c)

    for part in range(BLOCK // CHUNK):
        at = part * CHUNK
        x = side_by_side(spec, at)
        _, a1, s1, a2, s2, damping, logistic = forward(
            x, w_in_t[...], b_in_c[...], w_mid_t[...], b_mid_c[...], w_out_t[...], b_out_c[...]
        )
        act_one[part] = a1
        slope_one[part] = s1
        act_two[part] = a2
        slope_two[part] = s2
        damped[part] = time_step * damping
        driven[part] = (-time_step) * x * logistic
        for i in range(CHUNK):
            d = step * BLOCK + at + i
            columns = slice(i * WIDTH, (i + 1) * WIDTH)
            up, c = upwind[pl.ds(d, 1), :], courant[pl.ds(d, 1), :]
            index = jnp.broadcast_to(up, (FREQS, WIDTH))
            own = spec[at + i]
            upstream = jnp.where(from_inside(index), gathered(own, index + HALO), 0.0)
            damp = time_step * damping[:, columns]
            inside[part, :, columns] = own - c * (own - upstream) - damp * own
            hot = one_hot(jnp.broadcast_to(up - HALO, (WIDTH, WIDTH)))
            sent[part, :, columns] = spread(c * cot[at + i], hot)


def weight_specs():
    fixed = lambda i: (0, 0)
    return [
        pl.BlockSpec((FREQS, HID), fixed),
        pl.BlockSpec((1, HID), fixed),
        pl.BlockSpec((HID, HID), fixed),
        pl.BlockSpec((1, HID), fixed),
        pl.BlockSpec((FREQS, HID), fixed),
        pl.BlockSpec((1, FREQS), fixed),
    ]


def weight_scratch():
    return [
        pltpu.VMEM((HID, FREQS), BF16),
        pltpu.VMEM((HID, HID), F32),
        pltpu.VMEM((HID, HID), BF16),
        pltpu.VMEM((HID, HID), F32),
        pltpu.VMEM((FREQS, HID), F32),
    ]


PARTS = DIRS // CHUNK
SPAN = CHUNK * WIDTH


def saved_specs():
    per = BLOCK // CHUNK
    hid = pl.BlockSpec((per, HID, SPAN), lambda i: (i, 0, 0))
    freq = pl.BlockSpec((per, FREQS, SPAN), lambda i: (i, 0, 0))
    return [hid, hid, hid, hid, freq, freq, freq, freq]


def directions(rows=FREQS):
    return pl.BlockSpec((BLOCK, rows, WIDTH), lambda i: (i, 0, 0))


def whole_rows():
    return pl.BlockSpec((DIRS, WIDTH), lambda i: (0, 0))


def forward_saved(field, cotangent, courant, upwind, weights):
    hid = lambda kind: jax.ShapeDtypeStruct((PARTS, HID, SPAN), kind)
    freq = jax.ShapeDtypeStruct((PARTS, FREQS, SPAN), F32)
    return pl.pallas_call(
        forward_kernel,
        grid=(DIRS // BLOCK,),
        in_specs=[directions(), directions(), whole_rows(), whole_rows()] + weight_specs(),
        out_specs=saved_specs(),
        out_shape=[hid(BF16), hid(F32), hid(BF16), hid(F32), freq, freq, freq, freq],
        scratch_shapes=weight_scratch(),
        compiler_params=pltpu.CompilerParams(vmem_limit_bytes=LIMIT),
        cost_estimate=pl.CostEstimate(
            flops=2 * 24576 * DIRS * WIDTH, bytes_accessed=9_000_000, transcendentals=2 * HID * DIRS * WIDTH
        ),
        name="forward_start",
    )(*in_hbm(field, cotangent, courant, upwind, *weights))


def adjoint(incoming, driven, slope_one, slope_two, w_mid, w_out):
    g_source = (incoming * driven).astype(BF16)
    back_two = (dot(w_out, g_source) * slope_two).astype(BF16)
    back_one = (dot(w_mid, back_two) * slope_one).astype(BF16)
    return g_source, back_two, back_one


def main_kernel(
    spec, cot, courant, upwind, far, near, far_tail, near_tail,
    act_one, slope_one, act_two, slope_two, damped, driven, inside, sent,
    w_in, b_in, w_mid, b_mid, w_out_t, b_out,
    middle_out, back_out, grads,
    w_in_t, b_in_c, w_mid_t, b_mid_c, b_out_c, w_out, b_out_sum, rim_cs, rim_us, inner_sum, outer_sum,
):
    step = pl.program_id(0)

    @pl.when(step == 0)
    def _():
        set_weights(
            w_in, b_in, w_mid, b_mid, w_out_t, b_out, w_in_t, b_in_c, w_mid_t, b_mid_c, b_out_c, w_out
        )
        set_rim(far_tail, near_tail, rim_cs, rim_us)
        inner_sum[...] = jnp.zeros_like(inner_sum)
        outer_sum[...] = jnp.zeros_like(outer_sum)
        b_out_sum[...] = jnp.zeros_like(b_out_sum)

    odd = is_odd()
    sides = (lanes((FREQS, WIDTH)) < HALO).astype(jnp.int32)
    far_side = jnp.where(odd, 1 - sides, sides) == 1
    for part in range(BLOCK // CHUNK):
        at = part * CHUNK
        outside, courants, from_rim = [], [], []
        for i in range(CHUNK):
            d = step * BLOCK + at + i
            rows = slice((at + i) * FREQS, (at + i + 1) * FREQS)
            rim_x = jnp.where(far_side, far[rows], near[rows])
            rim_g = jnp.where(far_side, near[rows], far[rows])
            index = jnp.broadcast_to(upwind[pl.ds(d, 1), :], (FREQS, WIDTH))
            c = jnp.broadcast_to(courant[pl.ds(d, 1), :], (FREQS, WIDTH))
            outside.append(jnp.where(from_inside(index), 0.0, c * gathered(rim_x, index)))
            courants.append(c)
            rim_c, rim_u = rim_cs[pl.ds(d, 1), :], rim_us[pl.ds(d, 1), :]
            from_rim.append(spread(rim_c * rim_g, one_hot(jnp.broadcast_to(rim_u, (WIDTH, WIDTH)))))
        x = side_by_side(spec, at)
        g = side_by_side(cot, at)
        c = jnp.concatenate(courants, axis=1)
        field = inside[part] + jnp.concatenate(outside, axis=1)
        rounded, a1, s1, a2, s2, damping, logistic = forward(
            field, w_in_t[...], b_in_c[...], w_mid_t[...], b_mid_c[...], w_out_t[...], b_out_c[...]
        )
        gs, q2, q1 = adjoint(g, (-time_step) * field * logistic, s1, s2, w_mid[...], w_out[...])
        middle = (
            g * (1.0 - c - time_step * damping)
            + dot(w_in[...], q1)
            + sent[part]
            + jnp.concatenate(from_rim, axis=1)
        )
        gs_0, q2_0, q1_0 = adjoint(
            middle, driven[part], slope_one[part], slope_two[part], w_mid[...], w_out[...]
        )
        put_apart(middle_out, at, middle)
        back_out[part] = q1_0
        ones = jnp.ones((16, SPAN), BF16)
        left = jnp.concatenate([a1, rounded, ones], axis=0)
        left_0 = jnp.concatenate([act_one[part], x.astype(BF16), ones], axis=0)
        right, right_0 = jnp.concatenate([q2, q1], axis=0), jnp.concatenate([q2_0, q1_0], axis=0)
        inner_sum[...] += dot_nt(
            jnp.concatenate([left, left_0], axis=1), jnp.concatenate([right, right_0], axis=1)
        )
        outer_sum[...] += dot_nt(
            jnp.concatenate([gs, gs_0], axis=0), jnp.concatenate([a2, act_two[part]], axis=0)
        )
        b_out_sum[...] += sum(
            value[:, i * WIDTH : (i + 1) * WIDTH].astype(F32) for i in range(CHUNK) for value in (gs, gs_0)
        )

    @pl.when(step == pl.num_programs(0) - 1)
    def _():
        grads[:128] = inner_sum[:128, :HID]
        grads[128:160] = inner_sum[128:160, HID:]
        grads[160:192] = outer_sum[:FREQS, :HID] + outer_sum[FREQS:, HID:]
        grads[192:] = jnp.zeros((ROWS - 192, WIDTH), F32)
        grads[192:193] = inner_sum[160:161, HID:]
        grads[193:194] = inner_sum[160:161, :HID]
        grads[194:195, :FREQS] = jnp.sum(b_out_sum[...].T, axis=0, keepdims=True)


def both_adjoints(field, cotangent, courant, upwind, far, near, saved, weights):
    halo = pl.BlockSpec((BLOCK * FREQS, WIDTH), lambda i: (i, 0))
    tail = pl.BlockSpec((TAIL, WIDTH), lambda i: (DIRS * FREQS // TAIL, 0))
    per = BLOCK // CHUNK
    return pl.pallas_call(
        main_kernel,
        grid=(DIRS // BLOCK,),
        in_specs=[directions(), directions(), whole_rows(), whole_rows(), halo, halo, tail, tail]
        + saved_specs()
        + weight_specs(),
        out_specs=[
            directions(),
            pl.BlockSpec((per, HID, SPAN), lambda i: (i, 0, 0)),
            pl.BlockSpec((ROWS, WIDTH), lambda i: (0, 0)),
        ],
        out_shape=[
            jax.ShapeDtypeStruct((DIRS, FREQS, WIDTH), F32),
            pltpu.HBM((PARTS, HID, SPAN), BF16),
            jax.ShapeDtypeStruct((ROWS, WIDTH), F32),
        ],
        scratch_shapes=weight_scratch()
        + [
            pltpu.VMEM((HID, FREQS), BF16),
            pltpu.VMEM((FREQS, WIDTH), F32),
            pltpu.VMEM((TAIL, WIDTH), F32),
            pltpu.VMEM((TAIL, WIDTH), jnp.int32),
            pltpu.VMEM((HID + FREQS + 16, 2 * HID), F32),
            pltpu.VMEM((2 * FREQS, 2 * HID), F32),
        ],
        compiler_params=pltpu.CompilerParams(vmem_limit_bytes=LIMIT),
        cost_estimate=pl.CostEstimate(
            flops=10 * 24576 * DIRS * WIDTH, bytes_accessed=14_000_000, transcendentals=2 * HID * DIRS * WIDTH
        ),
        name="both_adjoints",
    )(field, cotangent, courant, upwind, far, near, far, near, *saved, *weights)


def edge_kernel(middle, to_far, to_near):
    odd = is_odd()
    first, second = middle[:, : FREQS // 2, :], middle[:, FREQS // 2 :, :]
    to_next = low_lanes(turned(first), second)
    to_prev = low_lanes(first, turned(second))
    to_far[...] = jnp.where(odd, to_next, to_prev)
    to_near[...] = jnp.where(odd, to_prev, to_next)


def packed_edges(middle):
    half = jax.ShapeDtypeStruct((DIRS, FREQS // 2, WIDTH), F32)
    return pl.pallas_call(
        edge_kernel,
        out_shape=(half, half),
        compiler_params=pltpu.CompilerParams(vmem_limit_bytes=LIMIT),
        cost_estimate=pl.CostEstimate(flops=1_000_000, bytes_accessed=1_200_000, transcendentals=0),
        name="pack_edges",
    )(middle)


def last_kernel(
    middle, back, damped, w_in, courant, upwind, far, near, far_tail, near_tail, out, rim_cs, rim_us
):
    step = pl.program_id(0)

    @pl.when(step == 0)
    def _():
        set_rim(far_tail, near_tail, rim_cs, rim_us)

    odd = is_odd()
    for part in range(BLOCK // CHUNK):
        state_back = dot(w_in[...], back[part])
        for k in range(CHUNK):
            i = part * CHUNK + k
            d = step * BLOCK + i
            columns = slice(k * WIDTH, (k + 1) * WIDTH)
            low, high = jnp.where(odd, near[i], far[i]), jnp.where(odd, far[i], near[i])
            rim = jnp.concatenate([low_lanes(high, turned(low)), low_lanes(turned(high), low)], axis=0)
            rim_c, rim_u = rim_cs[pl.ds(d, 1), :], rim_us[pl.ds(d, 1), :]
            own_u = upwind[pl.ds(d, 1), :] - HALO
            hot = jnp.concatenate(
                [one_hot(jnp.broadcast_to(u, (WIDTH, WIDTH))) for u in (own_u, rim_u)], axis=1
            )
            c, m = courant[pl.ds(d, 1), :], middle[i]
            moved = jnp.concatenate([c * m, rim_c * rim], axis=1)
            kept = m * (1.0 - c - damped[part, :, columns])
            out[0, i] = kept + state_back[:, columns] + spread(moved, hot)


def last_state(middle, back, damped, w_in, courant, upwind, far, near, far_first, near_first):
    tail = pl.BlockSpec((TAIL, WIDTH), lambda i: (DIRS * FREQS // TAIL, 0))
    edges = directions(FREQS // 2)
    hid, freq = saved_specs()[0], saved_specs()[4]
    return pl.pallas_call(
        last_kernel,
        grid=(DIRS // BLOCK,),
        in_specs=[directions(), hid, freq, weight_specs()[0], whole_rows(), whole_rows()]
        + [edges, edges, tail, tail],
        out_specs=pl.BlockSpec((1, BLOCK, FREQS, WIDTH), lambda i: (0, i, 0, 0)),
        out_shape=jax.ShapeDtypeStruct((1, DIRS, FREQS, WIDTH), F32),
        scratch_shapes=[pltpu.VMEM((TAIL, WIDTH), F32), pltpu.VMEM((TAIL, WIDTH), jnp.int32)],
        compiler_params=pltpu.CompilerParams(vmem_limit_bytes=LIMIT),
        cost_estimate=pl.CostEstimate(
            flops=8 * FREQS * WIDTH * WIDTH * DIRS, bytes_accessed=4_000_000, transcendentals=0
        ),
        name="last_state",
    )(middle, *in_hbm(back), damped, w_in, courant, upwind, far, near, far_first, near_first)


def clip_kernel(whole, w_in, b_in, w_mid, b_mid, w_out_t, b_out):
    x = whole[...]
    squares = jnp.sum(x * x, keepdims=True)
    factor = clip_norm / jnp.maximum(jnp.sqrt(squares), clip_norm)
    w_mid[...] = x[:128] * factor
    w_in[...] = x[128:160] * factor
    w_out_t[...] = x[160:192] * factor
    b_in[...] = x[192:193] * factor
    b_mid[...] = x[193:194] * factor
    b_out[...] = x[194:195, :FREQS] * factor


def clipped(whole):
    shape = lambda *s: jax.ShapeDtypeStruct(s, F32)
    w_in, b_in, w_mid, b_mid, w_out_t, b_out = pl.pallas_call(
        clip_kernel,
        out_shape=[
            shape(FREQS, HID),
            shape(1, HID),
            shape(HID, HID),
            shape(1, HID),
            shape(FREQS, HID),
            shape(1, FREQS),
        ],
        compiler_params=pltpu.CompilerParams(vmem_limit_bytes=LIMIT),
        name="clip",
    )(whole)
    return (w_in, b_in[0], w_mid, b_mid[0], w_out_t.T, b_out[0])


def exchanged(blocks, groups):
    return lax.all_to_all(
        blocks, ("space", "case"), 0, 0, axis_index_groups=groups, tiled=True
    )


def copied(parts, copies):
    total = jnp.sum(parts, axis=0)
    return jnp.broadcast_to(total[None], (copies,) + total.shape)


def device_groups():
    spaces, cases = lax.axis_size("space"), lax.axis_size("case")
    grid = np.arange(spaces * cases).reshape(spaces // 32, 32, cases)
    layers = grid.transpose(0, 2, 1).reshape(-1, 32)
    columns = grid.transpose(1, 0, 2).reshape(32, -1)
    return layers.tolist(), columns.tolist()


def summed_everywhere(parts):
    layers, columns = device_groups()
    wide, deep = len(layers[0]), len(columns[0])
    parts = exchanged(parts.reshape(wide, ROWS // wide, WIDTH), layers)
    parts = exchanged(copied(parts, deep), columns)
    return exchanged(copied(parts, wide), layers).reshape(ROWS, WIDTH)


def by_pairs(far, near):
    count = lax.axis_size("space")
    swapped = lambda first: [
        pair for i in range(first, count - 1, 2) for pair in ((i, i + 1), (i + 1, i))
    ]
    return lax.ppermute(far, "space", swapped(1)), lax.ppermute(near, "space", swapped(0))


def shards(spectrum, cotangent, courant, upwind, w_in, b_in, w_mid, b_mid, w_out, b_out):
    weights = (w_in, b_in[None], w_mid, b_mid[None], w_out.T, b_out[None])
    field, incoming = spectrum[0], cotangent[0]
    far, near = by_pairs(*packed_halo(spectrum, cotangent, courant, upwind))
    saved = forward_saved(field, incoming, courant, upwind, weights)
    middle, back, grads = both_adjoints(
        field, incoming, courant, upwind, far, near, saved, weights
    )
    totals = clipped(summed_everywhere(grads))
    far_mid, near_mid = by_pairs(*packed_edges(middle))
    state = last_state(
        middle, back, saved[4], w_in, courant, upwind, far_mid, near_mid, far, near
    )
    return (state, *totals)


def solution(mesh):
    placed = (
        P("case", None, None, "space"),
        P("case", None, None, "space"),
        P(None, "space"),
        P(None, "space"),
        P(),
        P(),
        P(),
        P(),
        P(),
        P(),
    )
    return jax.shard_map(
        shards,
        mesh=mesh,
        in_specs=placed,
        out_specs=(P("case", None, None, "space"), P(), P(), P(), P(), P(), P()),
        check_vma=False,
    )
```

```python
import jax
import jax.numpy as jnp
import numpy as np
from jax import lax
from jax.experimental import pallas as pl
from jax.experimental.pallas import tpu as pltpu
from jax.sharding import PartitionSpec as P

DIRS = 36
FREQS = 32
HID = 128
HALO = 64
WIDTH = 128
TAIL = 48
CHUNK = 12
BLOCK = 12
ROWS = 256

time_step = 0.3
clip_norm = 100.0
F32 = jnp.float32
BF16 = jnp.bfloat16
LIMIT = 40 * 1024 * 1024


def dot(a, b):
    return jnp.dot(a, b, preferred_element_type=F32)


def dot_nt(a, b):
    return lax.dot_general(a, b, (((1,), (1,)), ((), ())), preferred_element_type=F32)


def lanes(shape):
    return lax.broadcasted_iota(jnp.int32, shape, len(shape) - 1)


def turned(x):
    return pltpu.roll(x, HALO, x.ndim - 1)


def low_lanes(a, b):
    return jnp.where(lanes(a.shape) < HALO, a, b)


def in_hbm(*arrays):
    return [pltpu.with_memory_space_constraint(x, pltpu.HBM) for x in arrays]


def is_odd():
    return lax.axis_index("space") % 2 == 1


def pack_kernel(spec, cot, courant, upwind, far, near):
    main = DIRS * FREQS
    sides = lanes((8, WIDTH)) < HALO
    mine = jnp.where(is_odd(), sides.astype(jnp.int32), 1 - sides.astype(jnp.int32))

    def put(rows, x, g):
        here = jnp.broadcast_to(mine[:1], x.shape) == 1
        x = turned(x)
        far[rows] = jnp.where(here, x, g)
        near[rows] = jnp.where(here, g, x)

    put(slice(0, main), spec[0].reshape(main, WIDTH), cot[0].reshape(main, WIDTH))
    put(slice(main, main + DIRS), upwind[...].astype(F32), courant[...])
    rest = jnp.zeros((TAIL - DIRS, WIDTH), F32)
    far[main + DIRS :] = rest
    near[main + DIRS :] = rest


def packed_halo(spectrum, cotangent, courant, upwind):
    out = jax.ShapeDtypeStruct((DIRS * FREQS + TAIL, WIDTH), F32)
    return pl.pallas_call(
        pack_kernel,
        out_shape=(out, out),
        compiler_params=pltpu.CompilerParams(vmem_limit_bytes=LIMIT),
        name="pack_halo",
    )(*in_hbm(spectrum, cotangent, courant, upwind))


def set_rim(far, near, rim_c, rim_u):
    odd = is_odd()
    below = jnp.where(odd, near[...], far[...])
    above = jnp.where(odd, far[...], near[...])
    rim_c[...] = low_lanes(above, below)
    own = turned(low_lanes(below, above))
    offset = jnp.where(lanes(own.shape) < HALO, WIDTH - HALO, -(HALO + WIDTH))
    rim_u[...] = own.astype(jnp.int32) + offset


def one_hot(target):
    place = lax.broadcasted_iota(jnp.int32, (WIDTH, WIDTH), 0)
    return jnp.where(place == target, 1.0, 0.0).astype(BF16)


def spread(value, hot):
    high = value.astype(BF16)
    low = (value - high.astype(F32)).astype(BF16)
    both = dot_nt(jnp.concatenate([high, low], axis=0), hot)
    return both[:FREQS] + both[FREQS:]


def gathered(x, index):
    return jnp.take_along_axis(x, index & (WIDTH - 1), axis=1, mode="promise_in_bounds")


def from_inside(index):
    return (index >= HALO) & (index < HALO + WIDTH)


def column(row):
    return jnp.broadcast_to(row, (HID, HID)).T


def wide(tile, width):
    return jnp.concatenate([tile] * (width // tile.shape[1]), axis=1)


def activated(pre):
    logistic = 0.5 + 0.5 * jnp.tanh(0.5 * pre)
    act = pre * logistic
    return act.astype(BF16), logistic + act * (1.0 - logistic)


def forward(x, w_in_t, b_in, w_mid_t, b_mid, w_out_t, b_out):
    width = x.shape[1]
    rounded = x.astype(BF16)
    act_one, slope_one = activated(dot(w_in_t, rounded) + wide(b_in, width))
    act_two, slope_two = activated(dot(w_mid_t, act_one) + wide(b_mid, width))
    source = dot(w_out_t, act_two) + wide(b_out, width)
    damping = jnp.maximum(source, 0.0) + jnp.log(1.0 + jnp.exp(-jnp.abs(source)))
    logistic = 0.5 + 0.5 * jnp.tanh(0.5 * source)
    return rounded, act_one, slope_one, act_two, slope_two, damping, logistic


def set_weights(w_in, b_in, w_mid, b_mid, w_out_t, b_out, w_in_t, b_in_c, w_mid_t, b_mid_c, b_out_c, w_out=None):
    w_in_t[...] = w_in[...].astype(F32).T.astype(BF16)
    w_mid_t[...] = w_mid[...].astype(F32).T.astype(BF16)
    b_in_c[...] = column(b_in[...])
    b_mid_c[...] = column(b_mid[...])
    row = jnp.broadcast_to(b_out[...], (HID, FREQS))
    b_out_c[...] = row.T
    if w_out is not None:
        w_out[...] = w_out_t[...].astype(F32).T.astype(BF16)


def side_by_side(ref, at):
    return jnp.concatenate([ref[at + i] for i in range(CHUNK)], axis=1)


def put_apart(ref, at, value):
    for i in range(CHUNK):
        ref[at + i] = value[:, i * WIDTH : (i + 1) * WIDTH]


def forward_kernel(
    spec, cot, courant, upwind, w_in, b_in, w_mid, b_mid, w_out_t, b_out,
    act_one, slope_one, act_two, slope_two, damped, driven, inside, sent,
    w_in_t, b_in_c, w_mid_t, b_mid_c, b_out_c,
):
    step = pl.program_id(0)

    @pl.when(step == 0)
    def _():
        set_weights(w_in, b_in, w_mid, b_mid, w_out_t, b_out, w_in_t, b_in_c, w_mid_t, b_mid_c, b_out_c)

    for part in range(BLOCK // CHUNK):
        at = part * CHUNK
        x = side_by_side(spec, at)
        _, a1, s1, a2, s2, damping, logistic = forward(
            x, w_in_t[...], b_in_c[...], w_mid_t[...], b_mid_c[...], w_out_t[...], b_out_c[...]
        )
        act_one[part] = a1
        slope_one[part] = s1
        act_two[part] = a2
        slope_two[part] = s2
        damped[part] = time_step * damping
        driven[part] = (-time_step) * x * logistic
        for i in range(CHUNK):
            d = step * BLOCK + at + i
            columns = slice(i * WIDTH, (i + 1) * WIDTH)
            up, c = upwind[pl.ds(d, 1), :], courant[pl.ds(d, 1), :]
            index = jnp.broadcast_to(up, (FREQS, WIDTH))
            own = spec[at + i]
            upstream = jnp.where(from_inside(index), gathered(own, index + HALO), 0.0)
            damp = time_step * damping[:, columns]
            inside[part, :, columns] = own - c * (own - upstream) - damp * own
            hot = one_hot(jnp.broadcast_to(up - HALO, (WIDTH, WIDTH)))
            sent[part, :, columns] = spread(c * cot[at + i], hot)


def weight_specs():
    fixed = lambda i: (0, 0)
    return [
        pl.BlockSpec((FREQS, HID), fixed),
        pl.BlockSpec((1, HID), fixed),
        pl.BlockSpec((HID, HID), fixed),
        pl.BlockSpec((1, HID), fixed),
        pl.BlockSpec((FREQS, HID), fixed),
        pl.BlockSpec((1, FREQS), fixed),
    ]


def weight_scratch():
    return [
        pltpu.VMEM((HID, FREQS), BF16),
        pltpu.VMEM((HID, HID), F32),
        pltpu.VMEM((HID, HID), BF16),
        pltpu.VMEM((HID, HID), F32),
        pltpu.VMEM((FREQS, HID), F32),
    ]


PARTS = DIRS // CHUNK
SPAN = CHUNK * WIDTH


def saved_specs():
    per = BLOCK // CHUNK
    hid = pl.BlockSpec((per, HID, SPAN), lambda i: (i, 0, 0))
    freq = pl.BlockSpec((per, FREQS, SPAN), lambda i: (i, 0, 0))
    return [hid, hid, hid, hid, freq, freq, freq, freq]


def directions(rows=FREQS):
    return pl.BlockSpec((BLOCK, rows, WIDTH), lambda i: (i, 0, 0))


def whole_rows():
    return pl.BlockSpec((DIRS, WIDTH), lambda i: (0, 0))


def forward_saved(field, cotangent, courant, upwind, weights):
    hid = lambda kind: jax.ShapeDtypeStruct((PARTS, HID, SPAN), kind)
    freq = jax.ShapeDtypeStruct((PARTS, FREQS, SPAN), F32)
    return pl.pallas_call(
        forward_kernel,
        grid=(DIRS // BLOCK,),
        in_specs=[directions(), directions(), whole_rows(), whole_rows()] + weight_specs(),
        out_specs=saved_specs(),
        out_shape=[hid(BF16), hid(F32), hid(BF16), hid(F32), freq, freq, freq, freq],
        scratch_shapes=weight_scratch(),
        compiler_params=pltpu.CompilerParams(vmem_limit_bytes=LIMIT),
        cost_estimate=pl.CostEstimate(
            flops=2 * 24576 * DIRS * WIDTH, bytes_accessed=9_000_000, transcendentals=2 * HID * DIRS * WIDTH
        ),
        name="forward_start",
    )(*in_hbm(field, cotangent, courant, upwind, *weights))


def adjoint(incoming, rounded, driven, a1, s1, a2, s2, w_mid, w_out, grads, b_out_sum):
    width = incoming.shape[1]
    ones = jnp.ones((16, width), BF16)
    g_source = (incoming * driven).astype(BF16)
    grads[160:192] += dot_nt(g_source, a2)
    b_out_sum[...] += sum(
        g_source[:, i * WIDTH : (i + 1) * WIDTH].astype(F32) for i in range(width // WIDTH)
    )
    back_two = (dot(w_out, g_source) * s2).astype(BF16)
    grad = dot_nt(jnp.concatenate([a1, ones], axis=0), back_two)
    grads[:128] += grad[:128]
    grads[193:194] += grad[128:129]
    back_one = (dot(w_mid, back_two) * s1).astype(BF16)
    grad = dot_nt(jnp.concatenate([rounded, ones], axis=0), back_one)
    grads[128:160] += grad[:32]
    grads[192:193] += grad[32:33]
    return back_one


def main_kernel(
    spec, cot, courant, upwind, far, near,
    act_one, slope_one, act_two, slope_two, damped, driven, inside, sent,
    w_in, b_in, w_mid, b_mid, w_out_t, b_out,
    middle_out, back_out, grads,
    w_in_t, b_in_c, w_mid_t, b_mid_c, b_out_c, w_out, b_out_sum, rim_cs, rim_us,
):
    step = pl.program_id(0)

    @pl.when(step == 0)
    def _():
        set_weights(
            w_in, b_in, w_mid, b_mid, w_out_t, b_out, w_in_t, b_in_c, w_mid_t, b_mid_c, b_out_c, w_out
        )
        tail = pl.ds(DIRS * FREQS, TAIL)
        set_rim(far.at[tail], near.at[tail], rim_cs, rim_us)
        grads[...] = jnp.zeros_like(grads)
        b_out_sum[...] = jnp.zeros_like(b_out_sum)

    odd = is_odd()
    sides = (lanes((FREQS, WIDTH)) < HALO).astype(jnp.int32)

    for k in range(BLOCK // CHUNK):
        part = step * (BLOCK // CHUNK) + k
        far_side = jnp.where(odd, 1 - sides, sides) == 1
        at = part * CHUNK
        outside, courants, from_rim = [], [], []
        for i in range(CHUNK):
            d = at + i
            rows = pl.ds(pl.multiple_of(d * FREQS, FREQS), FREQS)
            far_d, near_d = far[rows, :], near[rows, :]
            rim_x = jnp.where(far_side, far_d, near_d)
            rim_g = jnp.where(far_side, near_d, far_d)
            index = jnp.broadcast_to(upwind[pl.ds(d, 1), :], (FREQS, WIDTH))
            c = jnp.broadcast_to(courant[pl.ds(d, 1), :], (FREQS, WIDTH))
            outside.append(jnp.where(from_inside(index), 0.0, c * gathered(rim_x, index)))
            courants.append(c)
            rim_c, rim_u = rim_cs[pl.ds(d, 1), :], rim_us[pl.ds(d, 1), :]
            from_rim.append(spread(rim_c * rim_g, one_hot(jnp.broadcast_to(rim_u, (WIDTH, WIDTH)))))
        x = side_by_side(spec, at)
        g = side_by_side(cot, at)
        c = jnp.concatenate(courants, axis=1)
        field = inside[part] + jnp.concatenate(outside, axis=1)
        rounded, a1, s1, a2, s2, damping, logistic = forward(
            field, w_in_t[...], b_in_c[...], w_mid_t[...], b_mid_c[...], w_out_t[...], b_out_c[...]
        )
        q1 = adjoint(
            g, rounded, (-time_step) * field * logistic, a1, s1, a2, s2,
            w_mid[...], w_out[...], grads, b_out_sum,
        )
        middle = (
            g * (1.0 - c - time_step * damping)
            + dot(w_in[...], q1)
            + sent[part]
            + jnp.concatenate(from_rim, axis=1)
        )
        put_apart(middle_out, k * CHUNK, middle)
        back_out[k] = adjoint(
            middle, x.astype(BF16), driven[part], act_one[part], slope_one[part], act_two[part],
            slope_two[part], w_mid[...], w_out[...], grads, b_out_sum,
        )

    @pl.when(step == pl.num_programs(0) - 1)
    def _():
        grads[194:195, :FREQS] = jnp.sum(b_out_sum[...].T, axis=0, keepdims=True)


def both_adjoints(field, cotangent, courant, upwind, far, near, saved, weights):
    return pl.pallas_call(
        main_kernel,
        grid=(DIRS // BLOCK,),
        in_specs=[pl.BlockSpec(memory_space=pltpu.VMEM)] * 20,
        out_specs=[
            directions(),
            pl.BlockSpec((BLOCK // CHUNK, HID, SPAN), lambda i: (i, 0, 0)),
            pl.BlockSpec((ROWS, WIDTH), lambda i: (0, 0)),
        ],
        out_shape=[
            jax.ShapeDtypeStruct((DIRS, FREQS, WIDTH), F32),
            pltpu.HBM((PARTS, HID, SPAN), BF16),
            jax.ShapeDtypeStruct((ROWS, WIDTH), F32),
        ],
        scratch_shapes=weight_scratch()
        + [
            pltpu.VMEM((HID, FREQS), BF16),
            pltpu.VMEM((FREQS, WIDTH), F32),
            pltpu.VMEM((TAIL, WIDTH), F32),
            pltpu.VMEM((TAIL, WIDTH), jnp.int32),
        ],
        compiler_params=pltpu.CompilerParams(vmem_limit_bytes=LIMIT),
        cost_estimate=pl.CostEstimate(
            flops=10 * 24576 * DIRS * WIDTH, bytes_accessed=14_000_000, transcendentals=2 * HID * DIRS * WIDTH
        ),
        name="both_adjoints",
    )(field, cotangent, courant, upwind, far, near, *saved, *weights)


def edge_kernel(middle, to_far, to_near):
    odd = is_odd()
    first, second = middle[:, : FREQS // 2, :], middle[:, FREQS // 2 :, :]
    to_next = low_lanes(turned(first), second)
    to_prev = low_lanes(first, turned(second))
    to_far[...] = jnp.where(odd, to_next, to_prev)
    to_near[...] = jnp.where(odd, to_prev, to_next)


def packed_edges(middle):
    half = jax.ShapeDtypeStruct((DIRS, FREQS // 2, WIDTH), F32)
    return pl.pallas_call(
        edge_kernel,
        out_shape=(half, half),
        compiler_params=pltpu.CompilerParams(vmem_limit_bytes=LIMIT),
        cost_estimate=pl.CostEstimate(flops=1_000_000, bytes_accessed=1_200_000, transcendentals=0),
        name="pack_edges",
    )(middle)


def last_kernel(
    middle, back, damped, w_in, courant, upwind, far, near, far_tail, near_tail, out, rim_cs, rim_us
):
    step = pl.program_id(0)

    @pl.when(step == 0)
    def _():
        set_rim(far_tail, near_tail, rim_cs, rim_us)

    odd = is_odd()
    for part in range(BLOCK // CHUNK):
        state_back = dot(w_in[...], back[part])
        for k in range(CHUNK):
            i = part * CHUNK + k
            d = step * BLOCK + i
            columns = slice(k * WIDTH, (k + 1) * WIDTH)
            low, high = jnp.where(odd, near[i], far[i]), jnp.where(odd, far[i], near[i])
            rim = jnp.concatenate([low_lanes(high, turned(low)), low_lanes(turned(high), low)], axis=0)
            rim_c, rim_u = rim_cs[pl.ds(d, 1), :], rim_us[pl.ds(d, 1), :]
            own_u = upwind[pl.ds(d, 1), :] - HALO
            hot = jnp.concatenate(
                [one_hot(jnp.broadcast_to(u, (WIDTH, WIDTH))) for u in (own_u, rim_u)], axis=1
            )
            c, m = courant[pl.ds(d, 1), :], middle[i]
            moved = jnp.concatenate([c * m, rim_c * rim], axis=1)
            kept = m * (1.0 - c - damped[part, :, columns])
            out[0, i] = kept + state_back[:, columns] + spread(moved, hot)


def last_state(middle, back, damped, w_in, courant, upwind, far, near, far_first, near_first):
    tail = pl.BlockSpec((TAIL, WIDTH), lambda i: (DIRS * FREQS // TAIL, 0))
    edges = directions(FREQS // 2)
    hid, freq = saved_specs()[0], saved_specs()[4]
    return pl.pallas_call(
        last_kernel,
        grid=(DIRS // BLOCK,),
        in_specs=[directions(), hid, freq, weight_specs()[0], whole_rows(), whole_rows()]
        + [edges, edges, tail, tail],
        out_specs=pl.BlockSpec((1, BLOCK, FREQS, WIDTH), lambda i: (0, i, 0, 0)),
        out_shape=jax.ShapeDtypeStruct((1, DIRS, FREQS, WIDTH), F32),
        scratch_shapes=[pltpu.VMEM((TAIL, WIDTH), F32), pltpu.VMEM((TAIL, WIDTH), jnp.int32)],
        compiler_params=pltpu.CompilerParams(vmem_limit_bytes=LIMIT),
        cost_estimate=pl.CostEstimate(
            flops=8 * FREQS * WIDTH * WIDTH * DIRS, bytes_accessed=4_000_000, transcendentals=0
        ),
        name="last_state",
    )(middle, *in_hbm(back), damped, w_in, courant, upwind, far, near, far_first, near_first)


def clip_kernel(whole, w_in, b_in, w_mid, b_mid, w_out_t, b_out):
    x = whole[...]
    squares = jnp.sum(x * x, keepdims=True)
    factor = clip_norm / jnp.maximum(jnp.sqrt(squares), clip_norm)
    w_mid[...] = x[:128] * factor
    w_in[...] = x[128:160] * factor
    w_out_t[...] = x[160:192] * factor
    b_in[...] = x[192:193] * factor
    b_mid[...] = x[193:194] * factor
    b_out[...] = x[194:195, :FREQS] * factor


def clipped(whole):
    shape = lambda *s: jax.ShapeDtypeStruct(s, F32)
    w_in, b_in, w_mid, b_mid, w_out_t, b_out = pl.pallas_call(
        clip_kernel,
        out_shape=[
            shape(FREQS, HID),
            shape(1, HID),
            shape(HID, HID),
            shape(1, HID),
            shape(FREQS, HID),
            shape(1, FREQS),
        ],
        compiler_params=pltpu.CompilerParams(vmem_limit_bytes=LIMIT),
        name="clip",
    )(whole)
    return (w_in, b_in[0], w_mid, b_mid[0], w_out_t.T, b_out[0])


def exchanged(blocks, groups):
    return lax.all_to_all(
        blocks, ("space", "case"), 0, 0, axis_index_groups=groups, tiled=True
    )


def copied(parts, copies):
    total = jnp.sum(parts, axis=0)
    return jnp.broadcast_to(total[None], (copies,) + total.shape)


def device_groups():
    spaces, cases = lax.axis_size("space"), lax.axis_size("case")
    ids = np.arange(spaces * cases).reshape(4, 2, 2, 2, 2, 2, cases)
    ids = ids.transpose(1, 3, 6, 0, 2, 4, 5).reshape(-1, 32)
    return ids.tolist(), ids.reshape(2, 2, cases, 32).reshape(-1, 32).T.tolist()


def by_pairs(far, near):
    count = lax.axis_size("space")
    swapped = lambda first: [
        pair for i in range(first, count - 1, 2) for pair in ((i, i + 1), (i + 1, i))
    ]
    return lax.ppermute(far, "space", swapped(1)), lax.ppermute(near, "space", swapped(0))


def shards(spectrum, cotangent, courant, upwind, w_in, b_in, w_mid, b_mid, w_out, b_out):
    weights = (w_in, b_in[None], w_mid, b_mid[None], w_out.T, b_out[None])
    field, incoming = spectrum[0], cotangent[0]
    far, near = by_pairs(*packed_halo(spectrum, cotangent, courant, upwind))
    saved = forward_saved(field, incoming, courant, upwind, weights)
    middle, back, grads = both_adjoints(
        field, incoming, courant, upwind, far, near, saved, weights
    )
    blocks, alike = device_groups()
    parts = exchanged(grads.reshape(len(blocks[0]), -1, WIDTH), blocks)
    parts = exchanged(copied(parts, len(alike[0])), alike)
    far_mid, near_mid = by_pairs(*packed_edges(middle))
    parts = copied(parts, len(blocks[0]))
    parts, far_mid, near_mid = lax.optimization_barrier((parts, far_mid, near_mid))
    totals = clipped(exchanged(parts, blocks).reshape(ROWS, WIDTH))
    state = last_state(
        middle, back, saved[4], w_in, courant, upwind, far_mid, near_mid, far, near
    )
    return (state, *totals)


def solution(mesh):
    placed = (
        P("case", None, None, "space"),
        P("case", None, None, "space"),
        P(None, "space"),
        P(None, "space"),
        P(),
        P(),
        P(),
        P(),
        P(),
        P(),
    )
    return jax.shard_map(
        shards,
        mesh=mesh,
        in_specs=placed,
        out_specs=(P("case", None, None, "space"), P(), P(), P(), P(), P(), P()),
        check_vma=False,
    )
```

```python
import jax
import jax.numpy as jnp
import numpy as np
from jax import lax
from jax.experimental import pallas as pl
from jax.experimental.pallas import tpu as pltpu
from jax.sharding import PartitionSpec as P

DIRS = 36
FREQS = 32
HID = 128
HALO = 64
WIDTH = 128
TAIL = 48
CHUNK = 12
HALF = 6
BLOCK = 12
ROWS = 256

time_step = 0.3
clip_norm = 100.0
F32 = jnp.float32
BF16 = jnp.bfloat16
LIMIT = 40 * 1024 * 1024


def dot(a, b):
    return jnp.dot(a, b, preferred_element_type=F32)


def dot_nt(a, b):
    return lax.dot_general(a, b, (((1,), (1,)), ((), ())), preferred_element_type=F32)


def lanes(shape):
    return lax.broadcasted_iota(jnp.int32, shape, len(shape) - 1)


def turned(x):
    return pltpu.roll(x, HALO, x.ndim - 1)


def low_lanes(a, b):
    return jnp.where(lanes(a.shape) < HALO, a, b)


def in_hbm(*arrays):
    return [pltpu.with_memory_space_constraint(x, pltpu.HBM) for x in arrays]


def is_odd():
    return lax.axis_index("space") % 2 == 1


def pack_kernel(spec, cot, courant, upwind, far, near):
    main = DIRS * FREQS
    sides = lanes((8, WIDTH)) < HALO
    mine = jnp.where(is_odd(), sides.astype(jnp.int32), 1 - sides.astype(jnp.int32))

    def put(rows, x, g):
        here = jnp.broadcast_to(mine[:1], x.shape) == 1
        x = turned(x)
        far[rows] = jnp.where(here, x, g)
        near[rows] = jnp.where(here, g, x)

    put(slice(0, main), spec[0].reshape(main, WIDTH), cot[0].reshape(main, WIDTH))
    put(slice(main, main + DIRS), upwind[...].astype(F32), courant[...])
    rest = jnp.zeros((TAIL - DIRS, WIDTH), F32)
    far[main + DIRS :] = rest
    near[main + DIRS :] = rest


def packed_halo(spectrum, cotangent, courant, upwind):
    out = jax.ShapeDtypeStruct((DIRS * FREQS + TAIL, WIDTH), F32)
    return pl.pallas_call(
        pack_kernel,
        out_shape=(out, out),
        compiler_params=pltpu.CompilerParams(vmem_limit_bytes=LIMIT),
        name="pack_halo",
    )(*in_hbm(spectrum, cotangent, courant, upwind))


def set_rim(far, near, rim_c, rim_u):
    odd = is_odd()
    below = jnp.where(odd, near[...], far[...])
    above = jnp.where(odd, far[...], near[...])
    rim_c[...] = low_lanes(above, below)
    own = turned(low_lanes(below, above))
    offset = jnp.where(lanes(own.shape) < HALO, WIDTH - HALO, -(HALO + WIDTH))
    rim_u[...] = own.astype(jnp.int32) + offset


def one_hot(target):
    place = lax.broadcasted_iota(jnp.int32, (WIDTH, WIDTH), 0)
    return jnp.where(place == target, 1.0, 0.0).astype(BF16)


def spread(value, hot):
    high = value.astype(BF16)
    low = (value - high.astype(F32)).astype(BF16)
    both = dot_nt(jnp.concatenate([high, low], axis=0), hot)
    return both[:FREQS] + both[FREQS:]


def gathered(x, index):
    return jnp.take_along_axis(x, index & (WIDTH - 1), axis=1, mode="promise_in_bounds")


def from_inside(index):
    return (index >= HALO) & (index < HALO + WIDTH)


def column(row):
    return jnp.broadcast_to(row, (HID, HID)).T


def wide(tile, width):
    return jnp.concatenate([tile] * (width // tile.shape[1]), axis=1)


def activated(pre):
    logistic = 0.5 + 0.5 * jnp.tanh(0.5 * pre)
    act = pre * logistic
    return act.astype(BF16), logistic + act * (1.0 - logistic)


def damping_of(source):
    damping = jnp.maximum(source, 0.0) + jnp.log(1.0 + jnp.exp(-jnp.abs(source)))
    return damping, 0.5 + 0.5 * jnp.tanh(0.5 * source)


def forward(x, w_in_t, b_in, w_mid_t, b_mid, w_out_t, b_out):
    width = x.shape[1]
    rounded = x.astype(BF16)
    act_one, slope_one = activated(dot(w_in_t, rounded) + wide(b_in, width))
    act_two, slope_two = activated(dot(w_mid_t, act_one) + wide(b_mid, width))
    source = dot(w_out_t, act_two) + wide(b_out, width)
    damping, logistic = damping_of(source)
    return rounded, act_one, slope_one, act_two, slope_two, damping, logistic


def set_weights(w_in, b_in, w_mid, b_mid, w_out_t, b_out, w_in_t, b_in_c, w_mid_t, b_mid_c, b_out_c, w_out=None):
    w_in_t[...] = w_in[...].astype(F32).T.astype(BF16)
    w_mid_t[...] = w_mid[...].astype(F32).T.astype(BF16)
    b_in_c[...] = column(b_in[...])
    b_mid_c[...] = column(b_mid[...])
    row = jnp.broadcast_to(b_out[...], (HID, FREQS))
    b_out_c[...] = row.T
    if w_out is not None:
        w_out[...] = w_out_t[...].astype(F32).T.astype(BF16)


def side_by_side(ref, at):
    return jnp.concatenate([ref[at + i] for i in range(CHUNK)], axis=1)


def put_apart(ref, at, value):
    for i in range(CHUNK):
        ref[at + i] = value[:, i * WIDTH : (i + 1) * WIDTH]


def forward_kernel(
    spec, cot, courant, upwind, w_in, b_in, w_mid, b_mid, w_out_t, b_out,
    act_one, slope_one, act_two, slope_two, damped, driven, inside, sent,
    w_in_t, b_in_c, w_mid_t, b_mid_c, b_out_c,
):
    step = pl.program_id(0)

    @pl.when(step == 0)
    def _():
        set_weights(w_in, b_in, w_mid, b_mid, w_out_t, b_out, w_in_t, b_in_c, w_mid_t, b_mid_c, b_out_c)

    for part in range(BLOCK // CHUNK):
        at = part * CHUNK
        x = side_by_side(spec, at)
        _, a1, s1, a2, s2, damping, logistic = forward(
            x, w_in_t[...], b_in_c[...], w_mid_t[...], b_mid_c[...], w_out_t[...], b_out_c[...]
        )
        act_one[part] = a1
        slope_one[part] = s1
        act_two[part] = a2
        slope_two[part] = s2
        damped[part] = time_step * damping
        driven[part] = (-time_step) * x * logistic
        for i in range(CHUNK):
            d = step * BLOCK + at + i
            columns = slice(i * WIDTH, (i + 1) * WIDTH)
            up, c = upwind[pl.ds(d, 1), :], courant[pl.ds(d, 1), :]
            index = jnp.broadcast_to(up, (FREQS, WIDTH))
            own = spec[at + i]
            upstream = jnp.where(from_inside(index), gathered(own, index + HALO), 0.0)
            damp = time_step * damping[:, columns]
            inside[part, :, columns] = own - c * (own - upstream) - damp * own
            hot = one_hot(jnp.broadcast_to(up - HALO, (WIDTH, WIDTH)))
            sent[part, :, columns] = spread(c * cot[at + i], hot)


def weight_specs():
    fixed = lambda i: (0, 0)
    return [
        pl.BlockSpec((FREQS, HID), fixed),
        pl.BlockSpec((1, HID), fixed),
        pl.BlockSpec((HID, HID), fixed),
        pl.BlockSpec((1, HID), fixed),
        pl.BlockSpec((FREQS, HID), fixed),
        pl.BlockSpec((1, FREQS), fixed),
    ]


def weight_scratch():
    return [
        pltpu.VMEM((HID, FREQS), BF16),
        pltpu.VMEM((HID, HID), F32),
        pltpu.VMEM((HID, HID), BF16),
        pltpu.VMEM((HID, HID), F32),
        pltpu.VMEM((FREQS, HID), F32),
    ]


PARTS = DIRS // CHUNK
SPAN = CHUNK * WIDTH


def saved_specs():
    per = BLOCK // CHUNK
    hid = pl.BlockSpec((per, HID, SPAN), lambda i: (i, 0, 0))
    freq = pl.BlockSpec((per, FREQS, SPAN), lambda i: (i, 0, 0))
    return [hid, hid, hid, hid, freq, freq, freq, freq]


def directions(rows=FREQS):
    return pl.BlockSpec((BLOCK, rows, WIDTH), lambda i: (i, 0, 0))


def whole_rows():
    return pl.BlockSpec((DIRS, WIDTH), lambda i: (0, 0))


def forward_saved(field, cotangent, courant, upwind, weights):
    hid = lambda kind: jax.ShapeDtypeStruct((PARTS, HID, SPAN), kind)
    freq = jax.ShapeDtypeStruct((PARTS, FREQS, SPAN), F32)
    return pl.pallas_call(
        forward_kernel,
        grid=(DIRS // BLOCK,),
        in_specs=[directions(), directions(), whole_rows(), whole_rows()] + weight_specs(),
        out_specs=saved_specs(),
        out_shape=[hid(BF16), hid(F32), hid(BF16), hid(F32), freq, freq, freq, freq],
        scratch_shapes=weight_scratch(),
        compiler_params=pltpu.CompilerParams(vmem_limit_bytes=LIMIT),
        cost_estimate=pl.CostEstimate(
            flops=2 * 24576 * DIRS * WIDTH, bytes_accessed=9_000_000, transcendentals=2 * HID * DIRS * WIDTH
        ),
        name="forward_start",
    )(*in_hbm(field, cotangent, courant, upwind, *weights))


def alternated(chains):
    waiting, running = list(chains), []
    while waiting or running:
        if waiting:
            running.append(waiting.pop(0))
        for chain in list(running):
            if next(chain, "done") == "done":
                running.remove(chain)


def main_kernel(
    spec, cot, courant, upwind, far, near, far_tail, near_tail,
    act_one, slope_one, act_two, slope_two, damped, driven, inside, sent,
    w_in, b_in, w_mid, b_mid, w_out_t, b_out,
    middle_out, back_out, grads,
    w_in_t, b_in_c, w_mid_t, b_mid_c, b_out_c, w_out, b_out_sum, rim_cs, rim_us,
):
    step = pl.program_id(0)

    @pl.when(step == 0)
    def _():
        set_weights(
            w_in, b_in, w_mid, b_mid, w_out_t, b_out, w_in_t, b_in_c, w_mid_t, b_mid_c, b_out_c, w_out
        )
        set_rim(far_tail, near_tail, rim_cs, rim_us)
        grads[...] = jnp.zeros_like(grads)
        b_out_sum[...] = jnp.zeros_like(b_out_sum)

    odd = is_odd()
    sides = (lanes((FREQS, WIDTH)) < HALO).astype(jnp.int32)
    far_side = jnp.where(odd, 1 - sides, sides) == 1
    ones = jnp.ones((16, HALF * WIDTH), BF16)

    def adjoint(incoming, rounded, driven_by, a1, s1, a2, s2, keep):
        g_source = (incoming * driven_by).astype(BF16)
        b_out_sum[...] += sum(
            g_source[:, i * WIDTH : (i + 1) * WIDTH].astype(F32) for i in range(HALF)
        )
        yield
        back = dot(w_out[...], g_source)
        grads[160:192] += dot_nt(g_source, a2)
        yield
        back_two = (back * s2).astype(BF16)
        yield
        back = dot(w_mid[...], back_two)
        grad = dot_nt(jnp.concatenate([a1, ones], axis=0), back_two)
        grads[:128] += grad[:128]
        grads[193:194] += grad[128:129]
        yield
        back_one = (back * s1).astype(BF16)
        yield
        grad = dot_nt(jnp.concatenate([rounded, ones], axis=0), back_one)
        grads[128:160] += grad[:32]
        grads[192:193] += grad[32:33]
        keep.append(back_one)

    def chain(at):
        columns = slice(at * WIDTH, (at + HALF) * WIDTH)
        outside, courants, from_rim = [], [], []
        for i in range(HALF):
            d = step * BLOCK + at + i
            rows = slice((at + i) * FREQS, (at + i + 1) * FREQS)
            rim_x = jnp.where(far_side, far[rows], near[rows])
            index = jnp.broadcast_to(upwind[pl.ds(d, 1), :], (FREQS, WIDTH))
            c = jnp.broadcast_to(courant[pl.ds(d, 1), :], (FREQS, WIDTH))
            outside.append(jnp.where(from_inside(index), 0.0, c * gathered(rim_x, index)))
            courants.append(c)
        c = jnp.concatenate(courants, axis=1)
        field = inside[0, :, columns] + jnp.concatenate(outside, axis=1)
        rounded = field.astype(BF16)
        yield
        pre = dot(w_in_t[...], rounded)
        yield
        a1, s1 = activated(pre + wide(b_in_c[...], HALF * WIDTH))
        yield
        pre = dot(w_mid_t[...], a1)
        yield
        a2, s2 = activated(pre + wide(b_mid_c[...], HALF * WIDTH))
        yield
        source = dot(w_out_t[...], a2)
        for i in range(HALF):
            d = step * BLOCK + at + i
            rows = slice((at + i) * FREQS, (at + i + 1) * FREQS)
            rim_g = jnp.where(far_side, near[rows], far[rows])
            rim_c, rim_u = rim_cs[pl.ds(d, 1), :], rim_us[pl.ds(d, 1), :]
            from_rim.append(spread(rim_c * rim_g, one_hot(jnp.broadcast_to(rim_u, (WIDTH, WIDTH)))))
        yield
        damping, logistic = damping_of(source + wide(b_out_c[...], HALF * WIDTH))
        g = jnp.concatenate([cot[at + i] for i in range(HALF)], axis=1)
        kept = []
        yield from adjoint(g, rounded, (-time_step) * field * logistic, a1, s1, a2, s2, kept)
        back = dot(w_in[...], kept[0])
        yield
        middle = (
            g * (1.0 - c - time_step * damping)
            + back
            + sent[0, :, columns]
            + jnp.concatenate(from_rim, axis=1)
        )
        for i in range(HALF):
            middle_out[at + i] = middle[:, i * WIDTH : (i + 1) * WIDTH]
        x = jnp.concatenate([spec[at + i] for i in range(HALF)], axis=1)
        yield from adjoint(
            middle, x.astype(BF16), driven[0, :, columns], act_one[0, :, columns],
            slope_one[0, :, columns], act_two[0, :, columns], slope_two[0, :, columns], kept,
        )
        back_out[0, :, columns] = kept[1]

    alternated(chain(at) for at in range(0, BLOCK, HALF))

    @pl.when(step == pl.num_programs(0) - 1)
    def _():
        grads[194:195, :FREQS] = jnp.sum(b_out_sum[...].T, axis=0, keepdims=True)


def both_adjoints(field, cotangent, courant, upwind, far, near, saved, weights):
    halo = pl.BlockSpec((BLOCK * FREQS, WIDTH), lambda i: (i, 0))
    tail = pl.BlockSpec((TAIL, WIDTH), lambda i: (DIRS * FREQS // TAIL, 0))
    per = BLOCK // CHUNK
    return pl.pallas_call(
        main_kernel,
        grid=(DIRS // BLOCK,),
        in_specs=[directions(), directions(), whole_rows(), whole_rows(), halo, halo, tail, tail]
        + saved_specs()
        + weight_specs(),
        out_specs=[
            directions(),
            pl.BlockSpec((per, HID, SPAN), lambda i: (i, 0, 0)),
            pl.BlockSpec((ROWS, WIDTH), lambda i: (0, 0)),
        ],
        out_shape=[
            jax.ShapeDtypeStruct((DIRS, FREQS, WIDTH), F32),
            pltpu.HBM((PARTS, HID, SPAN), BF16),
            jax.ShapeDtypeStruct((ROWS, WIDTH), F32),
        ],
        scratch_shapes=weight_scratch()
        + [
            pltpu.VMEM((HID, FREQS), BF16),
            pltpu.VMEM((FREQS, WIDTH), F32),
            pltpu.VMEM((TAIL, WIDTH), F32),
            pltpu.VMEM((TAIL, WIDTH), jnp.int32),
        ],
        compiler_params=pltpu.CompilerParams(vmem_limit_bytes=LIMIT),
        cost_estimate=pl.CostEstimate(
            flops=10 * 24576 * DIRS * WIDTH, bytes_accessed=14_000_000, transcendentals=2 * HID * DIRS * WIDTH
        ),
        name="both_adjoints",
    )(field, cotangent, courant, upwind, far, near, far, near, *saved, *weights)


def edge_kernel(middle, to_far, to_near):
    odd = is_odd()
    first, second = middle[:, : FREQS // 2, :], middle[:, FREQS // 2 :, :]
    to_next = low_lanes(turned(first), second)
    to_prev = low_lanes(first, turned(second))
    to_far[...] = jnp.where(odd, to_next, to_prev)
    to_near[...] = jnp.where(odd, to_prev, to_next)


def packed_edges(middle):
    half = jax.ShapeDtypeStruct((DIRS, FREQS // 2, WIDTH), F32)
    return pl.pallas_call(
        edge_kernel,
        out_shape=(half, half),
        compiler_params=pltpu.CompilerParams(vmem_limit_bytes=LIMIT),
        cost_estimate=pl.CostEstimate(flops=1_000_000, bytes_accessed=1_200_000, transcendentals=0),
        name="pack_edges",
    )(middle)


def last_kernel(
    middle, back, damped, w_in, courant, upwind, far, near, far_tail, near_tail, out, rim_cs, rim_us
):
    step = pl.program_id(0)

    @pl.when(step == 0)
    def _():
        set_rim(far_tail, near_tail, rim_cs, rim_us)

    odd = is_odd()
    for part in range(BLOCK // CHUNK):
        state_back = dot(w_in[...], back[part])
        for k in range(CHUNK):
            i = part * CHUNK + k
            d = step * BLOCK + i
            columns = slice(k * WIDTH, (k + 1) * WIDTH)
            low, high = jnp.where(odd, near[i], far[i]), jnp.where(odd, far[i], near[i])
            rim = jnp.concatenate([low_lanes(high, turned(low)), low_lanes(turned(high), low)], axis=0)
            rim_c, rim_u = rim_cs[pl.ds(d, 1), :], rim_us[pl.ds(d, 1), :]
            own_u = upwind[pl.ds(d, 1), :] - HALO
            hot = jnp.concatenate(
                [one_hot(jnp.broadcast_to(u, (WIDTH, WIDTH))) for u in (own_u, rim_u)], axis=1
            )
            c, m = courant[pl.ds(d, 1), :], middle[i]
            moved = jnp.concatenate([c * m, rim_c * rim], axis=1)
            kept = m * (1.0 - c - damped[part, :, columns])
            out[0, i] = kept + state_back[:, columns] + spread(moved, hot)


def last_state(middle, back, damped, w_in, courant, upwind, far, near, far_first, near_first):
    tail = pl.BlockSpec((TAIL, WIDTH), lambda i: (DIRS * FREQS // TAIL, 0))
    edges = directions(FREQS // 2)
    hid, freq = saved_specs()[0], saved_specs()[4]
    return pl.pallas_call(
        last_kernel,
        grid=(DIRS // BLOCK,),
        in_specs=[directions(), hid, freq, weight_specs()[0], whole_rows(), whole_rows()]
        + [edges, edges, tail, tail],
        out_specs=pl.BlockSpec((1, BLOCK, FREQS, WIDTH), lambda i: (0, i, 0, 0)),
        out_shape=jax.ShapeDtypeStruct((1, DIRS, FREQS, WIDTH), F32),
        scratch_shapes=[pltpu.VMEM((TAIL, WIDTH), F32), pltpu.VMEM((TAIL, WIDTH), jnp.int32)],
        compiler_params=pltpu.CompilerParams(vmem_limit_bytes=LIMIT),
        cost_estimate=pl.CostEstimate(
            flops=8 * FREQS * WIDTH * WIDTH * DIRS, bytes_accessed=4_000_000, transcendentals=0
        ),
        name="last_state",
    )(middle, *in_hbm(back), damped, w_in, courant, upwind, far, near, far_first, near_first)


def clip_kernel(whole, w_in, b_in, w_mid, b_mid, w_out_t, b_out):
    x = whole[...]
    squares = jnp.sum(x * x, keepdims=True)
    factor = clip_norm / jnp.maximum(jnp.sqrt(squares), clip_norm)
    w_mid[...] = x[:128] * factor
    w_in[...] = x[128:160] * factor
    w_out_t[...] = x[160:192] * factor
    b_in[...] = x[192:193] * factor
    b_mid[...] = x[193:194] * factor
    b_out[...] = x[194:195, :FREQS] * factor


def clipped(whole):
    shape = lambda *s: jax.ShapeDtypeStruct(s, F32)
    w_in, b_in, w_mid, b_mid, w_out_t, b_out = pl.pallas_call(
        clip_kernel,
        out_shape=[
            shape(FREQS, HID),
            shape(1, HID),
            shape(HID, HID),
            shape(1, HID),
            shape(FREQS, HID),
            shape(1, FREQS),
        ],
        compiler_params=pltpu.CompilerParams(vmem_limit_bytes=LIMIT),
        name="clip",
    )(whole)
    return (w_in, b_in[0], w_mid, b_mid[0], w_out_t.T, b_out[0])


def exchanged(blocks, groups):
    return lax.all_to_all(
        blocks, ("space", "case"), 0, 0, axis_index_groups=groups, tiled=True
    )


def copied(parts, copies):
    total = jnp.sum(parts, axis=0)
    return jnp.broadcast_to(total[None], (copies,) + total.shape)


def device_groups():
    spaces, cases = lax.axis_size("space"), lax.axis_size("case")
    grid = np.arange(spaces * cases).reshape(spaces // 32, 32, cases)
    layers = grid.transpose(0, 2, 1).reshape(-1, 32)
    columns = grid.transpose(1, 0, 2).reshape(32, -1)
    return layers.tolist(), columns.tolist()


def summed_everywhere(parts):
    layers, columns = device_groups()
    wide, deep = len(layers[0]), len(columns[0])
    parts = exchanged(parts.reshape(wide, ROWS // wide, WIDTH), layers)
    parts = exchanged(copied(parts, deep), columns)
    return exchanged(copied(parts, wide), layers).reshape(ROWS, WIDTH)


def by_pairs(far, near):
    count = lax.axis_size("space")
    swapped = lambda first: [
        pair for i in range(first, count - 1, 2) for pair in ((i, i + 1), (i + 1, i))
    ]
    return lax.ppermute(far, "space", swapped(1)), lax.ppermute(near, "space", swapped(0))


def shards(spectrum, cotangent, courant, upwind, w_in, b_in, w_mid, b_mid, w_out, b_out):
    weights = (w_in, b_in[None], w_mid, b_mid[None], w_out.T, b_out[None])
    field, incoming = spectrum[0], cotangent[0]
    far, near = by_pairs(*packed_halo(spectrum, cotangent, courant, upwind))
    saved = forward_saved(field, incoming, courant, upwind, weights)
    middle, back, grads = both_adjoints(
        field, incoming, courant, upwind, far, near, saved, weights
    )
    totals = clipped(summed_everywhere(grads))
    far_mid, near_mid = by_pairs(*packed_edges(middle))
    state = last_state(
        middle, back, saved[4], w_in, courant, upwind, far_mid, near_mid, far, near
    )
    return (state, *totals)


def solution(mesh):
    placed = (
        P("case", None, None, "space"),
        P("case", None, None, "space"),
        P(None, "space"),
        P(None, "space"),
        P(),
        P(),
        P(),
        P(),
        P(),
        P(),
    )
    return jax.shard_map(
        shards,
        mesh=mesh,
        in_specs=placed,
        out_specs=(P("case", None, None, "space"), P(), P(), P(), P(), P(), P()),
        check_vma=False,
    )
```

```python
import jax
import jax.numpy as jnp
import numpy as np
from jax import lax
from jax.experimental import pallas as pl
from jax.experimental.pallas import tpu as pltpu
from jax.sharding import PartitionSpec as P

DIRS = 36
FREQS = 32
HID = 128
HALO = 64
WIDTH = 128
TAIL = 48
CHUNK = 18
HALF = 18
BLOCK = 18
ROWS = 256

time_step = 0.3
clip_norm = 100.0
F32 = jnp.float32
BF16 = jnp.bfloat16
LIMIT = 40 * 1024 * 1024


def dot(a, b):
    return jnp.dot(a, b, preferred_element_type=F32)


def dot_nt(a, b):
    return lax.dot_general(a, b, (((1,), (1,)), ((), ())), preferred_element_type=F32)


def lanes(shape):
    return lax.broadcasted_iota(jnp.int32, shape, len(shape) - 1)


def turned(x):
    return pltpu.roll(x, HALO, x.ndim - 1)


def low_lanes(a, b):
    return jnp.where(lanes(a.shape) < HALO, a, b)


def in_hbm(*arrays):
    return [pltpu.with_memory_space_constraint(x, pltpu.HBM) for x in arrays]


def is_odd():
    return lax.axis_index("space") % 2 == 1


def pack_kernel(spec, cot, courant, upwind, far, near):
    main = DIRS * FREQS
    sides = lanes((8, WIDTH)) < HALO
    mine = jnp.where(is_odd(), sides.astype(jnp.int32), 1 - sides.astype(jnp.int32))

    def put(rows, x, g):
        here = jnp.broadcast_to(mine[:1], x.shape) == 1
        x = turned(x)
        far[rows] = jnp.where(here, x, g)
        near[rows] = jnp.where(here, g, x)

    put(slice(0, main), spec[0].reshape(main, WIDTH), cot[0].reshape(main, WIDTH))
    put(slice(main, main + DIRS), upwind[...].astype(F32), courant[...])
    rest = jnp.zeros((TAIL - DIRS, WIDTH), F32)
    far[main + DIRS :] = rest
    near[main + DIRS :] = rest


def packed_halo(spectrum, cotangent, courant, upwind):
    out = jax.ShapeDtypeStruct((DIRS * FREQS + TAIL, WIDTH), F32)
    return pl.pallas_call(
        pack_kernel,
        out_shape=(out, out),
        compiler_params=pltpu.CompilerParams(vmem_limit_bytes=LIMIT),
        name="pack_halo",
    )(*in_hbm(spectrum, cotangent, courant, upwind))


def set_rim(far, near, rim_c, rim_u):
    odd = is_odd()
    below = jnp.where(odd, near[...], far[...])
    above = jnp.where(odd, far[...], near[...])
    rim_c[...] = low_lanes(above, below)
    own = turned(low_lanes(below, above))
    offset = jnp.where(lanes(own.shape) < HALO, WIDTH - HALO, -(HALO + WIDTH))
    rim_u[...] = own.astype(jnp.int32) + offset


def one_hot(target):
    place = lax.broadcasted_iota(jnp.int32, (WIDTH, WIDTH), 0)
    return jnp.where(place == target, 1.0, 0.0).astype(BF16)


def spread(value, hot):
    high = value.astype(BF16)
    low = (value - high.astype(F32)).astype(BF16)
    both = dot_nt(jnp.concatenate([high, low], axis=0), hot)
    return both[:FREQS] + both[FREQS:]


def gathered(x, index):
    return jnp.take_along_axis(x, index & (WIDTH - 1), axis=1, mode="promise_in_bounds")


def from_inside(index):
    return (index >= HALO) & (index < HALO + WIDTH)


def column(row):
    return jnp.broadcast_to(row, (HID, HID)).T


def wide(tile, width):
    return jnp.concatenate([tile] * (width // tile.shape[1]), axis=1)


def activated(pre):
    logistic = 0.5 + 0.5 * jnp.tanh(0.5 * pre)
    act = pre * logistic
    return act.astype(BF16), logistic + act * (1.0 - logistic)


def damping_of(source):
    damping = jnp.maximum(source, 0.0) + jnp.log(1.0 + jnp.exp(-jnp.abs(source)))
    return damping, 0.5 + 0.5 * jnp.tanh(0.5 * source)


def forward(x, w_in_t, b_in, w_mid_t, b_mid, w_out_t, b_out):
    width = x.shape[1]
    rounded = x.astype(BF16)
    act_one, slope_one = activated(dot(w_in_t, rounded) + wide(b_in, width))
    act_two, slope_two = activated(dot(w_mid_t, act_one) + wide(b_mid, width))
    source = dot(w_out_t, act_two) + wide(b_out, width)
    damping, logistic = damping_of(source)
    return rounded, act_one, slope_one, act_two, slope_two, damping, logistic


def set_weights(w_in, b_in, w_mid, b_mid, w_out_t, b_out, w_in_t, b_in_c, w_mid_t, b_mid_c, b_out_c, w_out):
    w_in_t[...] = w_in[...].astype(F32).T.astype(BF16)
    w_mid_t[...] = w_mid[...].astype(F32).T.astype(BF16)
    b_in_c[...] = column(b_in[...])
    b_mid_c[...] = column(b_mid[...])
    row = jnp.broadcast_to(b_out[...], (HID, FREQS))
    b_out_c[...] = row.T
    w_out[...] = w_out_t[...].astype(F32).T.astype(BF16)


def side_by_side(ref, at):
    return jnp.concatenate([ref[at + i] for i in range(CHUNK)], axis=1)


def put_apart(ref, at, value):
    for i in range(CHUNK):
        ref[at + i] = value[:, i * WIDTH : (i + 1) * WIDTH]


def forward_kernel(
    spec, cot, courant, upwind, w_in, b_in, w_mid, b_mid, w_out_t, b_out,
    act_one, slope_one, act_two, slope_two, damped, driven, inside, sent,
    w_in_t, b_in_c, w_mid_t, b_mid_c, b_out_c, w_out,
):
    step = pl.program_id(0)

    @pl.when(step == 0)
    def _():
        set_weights(
            w_in, b_in, w_mid, b_mid, w_out_t, b_out, w_in_t, b_in_c, w_mid_t, b_mid_c, b_out_c, w_out
        )

    for part in range(BLOCK // CHUNK):
        at = part * CHUNK
        x = side_by_side(spec, at)
        _, a1, s1, a2, s2, damping, logistic = forward(
            x, w_in_t[...], b_in_c[...], w_mid_t[...], b_mid_c[...], w_out_t[...], b_out_c[...]
        )
        act_one[part] = a1
        slope_one[part] = s1
        act_two[part] = a2
        slope_two[part] = s2
        damped[part] = time_step * damping
        driven[part] = (-time_step) * x * logistic
        for i in range(CHUNK):
            d = step * BLOCK + at + i
            columns = slice(i * WIDTH, (i + 1) * WIDTH)
            up, c = upwind[pl.ds(d, 1), :], courant[pl.ds(d, 1), :]
            index = jnp.broadcast_to(up, (FREQS, WIDTH))
            own = spec[at + i]
            upstream = jnp.where(from_inside(index), gathered(own, index + HALO), 0.0)
            damp = time_step * damping[:, columns]
            inside[part, :, columns] = own - c * (own - upstream) - damp * own
            hot = one_hot(jnp.broadcast_to(up - HALO, (WIDTH, WIDTH)))
            sent[part, :, columns] = spread(c * cot[at + i], hot)


def weight_specs():
    fixed = lambda i: (0, 0)
    return [
        pl.BlockSpec((FREQS, HID), fixed),
        pl.BlockSpec((1, HID), fixed),
        pl.BlockSpec((HID, HID), fixed),
        pl.BlockSpec((1, HID), fixed),
        pl.BlockSpec((FREQS, HID), fixed),
        pl.BlockSpec((1, FREQS), fixed),
    ]


TURNED = (
    ((HID, FREQS), BF16),
    ((HID, HID), F32),
    ((HID, HID), BF16),
    ((HID, HID), F32),
    ((FREQS, HID), F32),
    ((HID, FREQS), BF16),
)


def turned_specs():
    return [pl.BlockSpec(shape, lambda i: (0, 0)) for shape, _ in TURNED]


PARTS = DIRS // CHUNK
SPAN = CHUNK * WIDTH


def saved_specs():
    per = BLOCK // CHUNK
    hid = pl.BlockSpec((per, HID, SPAN), lambda i: (i, 0, 0))
    freq = pl.BlockSpec((per, FREQS, SPAN), lambda i: (i, 0, 0))
    return [hid, hid, hid, hid, freq, freq, freq, freq]


def directions(rows=FREQS):
    return pl.BlockSpec((BLOCK, rows, WIDTH), lambda i: (i, 0, 0))


def whole_rows():
    return pl.BlockSpec((DIRS, WIDTH), lambda i: (0, 0))


def forward_saved(field, cotangent, courant, upwind, weights):
    hid = lambda kind: jax.ShapeDtypeStruct((PARTS, HID, SPAN), kind)
    freq = jax.ShapeDtypeStruct((PARTS, FREQS, SPAN), F32)
    return pl.pallas_call(
        forward_kernel,
        grid=(DIRS // BLOCK,),
        in_specs=[directions(), directions(), whole_rows(), whole_rows()] + weight_specs(),
        out_specs=saved_specs() + turned_specs(),
        out_shape=[hid(BF16), hid(F32), hid(BF16), hid(F32), freq, freq, freq, freq]
        + [jax.ShapeDtypeStruct(*item) for item in TURNED],
        compiler_params=pltpu.CompilerParams(vmem_limit_bytes=LIMIT),
        cost_estimate=pl.CostEstimate(
            flops=2 * 24576 * DIRS * WIDTH, bytes_accessed=9_000_000, transcendentals=2 * HID * DIRS * WIDTH
        ),
        name="forward_start",
    )(*in_hbm(field, cotangent, courant, upwind, *weights))


def alternated(chains):
    waiting, running = list(chains), []
    while waiting or running:
        if waiting:
            running.append(waiting.pop(0))
        for chain in list(running):
            if next(chain, "done") == "done":
                running.remove(chain)


def main_kernel(
    spec, cot, courant, upwind, far, near, far_tail, near_tail,
    act_one, slope_one, act_two, slope_two, damped, driven, inside, sent,
    w_in_t, b_in_c, w_mid_t, b_mid_c, b_out_c, w_out, w_in, w_mid, w_out_t,
    middle_out, back_out, grads,
    b_out_sum, rim_cs, rim_us,
):
    step = pl.program_id(0)

    @pl.when(step == 0)
    def _():
        set_rim(far_tail, near_tail, rim_cs, rim_us)
        grads[...] = jnp.zeros_like(grads)
        b_out_sum[...] = jnp.zeros_like(b_out_sum)

    odd = is_odd()
    sides = (lanes((FREQS, WIDTH)) < HALO).astype(jnp.int32)
    far_side = jnp.where(odd, 1 - sides, sides) == 1
    ones = jnp.ones((16, HALF * WIDTH), BF16)

    def adjoint(incoming, rounded, driven_by, a1, s1, a2, s2, keep):
        g_source = (incoming * driven_by).astype(BF16)
        b_out_sum[...] += sum(
            g_source[:, i * WIDTH : (i + 1) * WIDTH].astype(F32) for i in range(HALF)
        )
        yield
        back = dot(w_out[...], g_source)
        grads[160:192] += dot_nt(g_source, a2)
        yield
        back_two = (back * s2).astype(BF16)
        yield
        back = dot(w_mid[...], back_two)
        grad = dot_nt(jnp.concatenate([a1, ones], axis=0), back_two)
        grads[:128] += grad[:128]
        grads[193:194] += grad[128:129]
        yield
        back_one = (back * s1).astype(BF16)
        yield
        grad = dot_nt(jnp.concatenate([rounded, ones], axis=0), back_one)
        grads[128:160] += grad[:32]
        grads[192:193] += grad[32:33]
        keep.append(back_one)

    def chain(at):
        columns = slice(at * WIDTH, (at + HALF) * WIDTH)
        outside, courants, from_rim = [], [], []
        for i in range(HALF):
            d = step * BLOCK + at + i
            rows = slice((at + i) * FREQS, (at + i + 1) * FREQS)
            rim_x = jnp.where(far_side, far[rows], near[rows])
            index = jnp.broadcast_to(upwind[pl.ds(d, 1), :], (FREQS, WIDTH))
            c = jnp.broadcast_to(courant[pl.ds(d, 1), :], (FREQS, WIDTH))
            outside.append(jnp.where(from_inside(index), 0.0, c * gathered(rim_x, index)))
            courants.append(c)
        c = jnp.concatenate(courants, axis=1)
        field = inside[0, :, columns] + jnp.concatenate(outside, axis=1)
        rounded = field.astype(BF16)
        yield
        pre = dot(w_in_t[...], rounded)
        yield
        a1, s1 = activated(pre + wide(b_in_c[...], HALF * WIDTH))
        yield
        pre = dot(w_mid_t[...], a1)
        yield
        a2, s2 = activated(pre + wide(b_mid_c[...], HALF * WIDTH))
        yield
        source = dot(w_out_t[...], a2)
        for i in range(HALF):
            d = step * BLOCK + at + i
            rows = slice((at + i) * FREQS, (at + i + 1) * FREQS)
            rim_g = jnp.where(far_side, near[rows], far[rows])
            rim_c, rim_u = rim_cs[pl.ds(d, 1), :], rim_us[pl.ds(d, 1), :]
            from_rim.append(spread(rim_c * rim_g, one_hot(jnp.broadcast_to(rim_u, (WIDTH, WIDTH)))))
        yield
        damping, logistic = damping_of(source + wide(b_out_c[...], HALF * WIDTH))
        g = jnp.concatenate([cot[at + i] for i in range(HALF)], axis=1)
        kept = []
        yield from adjoint(g, rounded, (-time_step) * field * logistic, a1, s1, a2, s2, kept)
        back = dot(w_in[...], kept[0])
        yield
        middle = (
            g * (1.0 - c - time_step * damping)
            + back
            + sent[0, :, columns]
            + jnp.concatenate(from_rim, axis=1)
        )
        for i in range(HALF):
            middle_out[at + i] = middle[:, i * WIDTH : (i + 1) * WIDTH]
        x = jnp.concatenate([spec[at + i] for i in range(HALF)], axis=1)
        yield from adjoint(
            middle, x.astype(BF16), driven[0, :, columns], act_one[0, :, columns],
            slope_one[0, :, columns], act_two[0, :, columns], slope_two[0, :, columns], kept,
        )
        back_out[0, :, columns] = kept[1]

    alternated(chain(at) for at in range(0, BLOCK, HALF))

    @pl.when(step == pl.num_programs(0) - 1)
    def _():
        grads[194:195, :FREQS] = jnp.sum(b_out_sum[...].T, axis=0, keepdims=True)


def both_adjoints(field, cotangent, courant, upwind, far, near, saved, w_in, w_mid, w_out_t):
    halo = pl.BlockSpec((BLOCK * FREQS, WIDTH), lambda i: (i, 0))
    tail = pl.BlockSpec((TAIL, WIDTH), lambda i: (DIRS * FREQS // TAIL, 0))
    per = BLOCK // CHUNK
    return pl.pallas_call(
        main_kernel,
        grid=(DIRS // BLOCK,),
        in_specs=[directions(), directions(), whole_rows(), whole_rows(), halo, halo, tail, tail]
        + saved_specs()
        + turned_specs()
        + [weight_specs()[0], weight_specs()[2], weight_specs()[4]],
        out_specs=[
            directions(),
            pl.BlockSpec((per, HID, SPAN), lambda i: (i, 0, 0)),
            pl.BlockSpec((ROWS, WIDTH), lambda i: (0, 0)),
        ],
        out_shape=[
            jax.ShapeDtypeStruct((DIRS, FREQS, WIDTH), F32),
            pltpu.HBM((PARTS, HID, SPAN), BF16),
            jax.ShapeDtypeStruct((ROWS, WIDTH), F32),
        ],
        scratch_shapes=[
            pltpu.VMEM((FREQS, WIDTH), F32),
            pltpu.VMEM((TAIL, WIDTH), F32),
            pltpu.VMEM((TAIL, WIDTH), jnp.int32),
        ],
        compiler_params=pltpu.CompilerParams(vmem_limit_bytes=LIMIT),
        cost_estimate=pl.CostEstimate(
            flops=10 * 24576 * DIRS * WIDTH, bytes_accessed=14_000_000, transcendentals=2 * HID * DIRS * WIDTH
        ),
        name="both_adjoints",
    )(field, cotangent, courant, upwind, far, near, far, near, *saved, w_in, w_mid, w_out_t)


def edge_kernel(middle, to_far, to_near):
    odd = is_odd()
    first, second = middle[:, : FREQS // 2, :], middle[:, FREQS // 2 :, :]
    to_next = low_lanes(turned(first), second)
    to_prev = low_lanes(first, turned(second))
    to_far[...] = jnp.where(odd, to_next, to_prev)
    to_near[...] = jnp.where(odd, to_prev, to_next)


def packed_edges(middle):
    half = jax.ShapeDtypeStruct((DIRS, FREQS // 2, WIDTH), F32)
    return pl.pallas_call(
        edge_kernel,
        out_shape=(half, half),
        compiler_params=pltpu.CompilerParams(vmem_limit_bytes=LIMIT),
        cost_estimate=pl.CostEstimate(flops=1_000_000, bytes_accessed=1_200_000, transcendentals=0),
        name="pack_edges",
    )(middle)


def last_kernel(
    middle, back, damped, w_in, courant, upwind, far, near, far_tail, near_tail, out, rim_cs, rim_us
):
    step = pl.program_id(0)

    @pl.when(step == 0)
    def _():
        set_rim(far_tail, near_tail, rim_cs, rim_us)

    odd = is_odd()
    for part in range(BLOCK // CHUNK):
        state_back = dot(w_in[...], back[part])
        for k in range(CHUNK):
            i = part * CHUNK + k
            d = step * BLOCK + i
            columns = slice(k * WIDTH, (k + 1) * WIDTH)
            low, high = jnp.where(odd, near[i], far[i]), jnp.where(odd, far[i], near[i])
            rim = jnp.concatenate([low_lanes(high, turned(low)), low_lanes(turned(high), low)], axis=0)
            rim_c, rim_u = rim_cs[pl.ds(d, 1), :], rim_us[pl.ds(d, 1), :]
            own_u = upwind[pl.ds(d, 1), :] - HALO
            hot = jnp.concatenate(
                [one_hot(jnp.broadcast_to(u, (WIDTH, WIDTH))) for u in (own_u, rim_u)], axis=1
            )
            c, m = courant[pl.ds(d, 1), :], middle[i]
            moved = jnp.concatenate([c * m, rim_c * rim], axis=1)
            kept = m * (1.0 - c - damped[part, :, columns])
            out[0, i] = kept + state_back[:, columns] + spread(moved, hot)


def last_state(middle, back, damped, w_in, courant, upwind, far, near, far_first, near_first):
    tail = pl.BlockSpec((TAIL, WIDTH), lambda i: (DIRS * FREQS // TAIL, 0))
    edges = directions(FREQS // 2)
    hid, freq = saved_specs()[0], saved_specs()[4]
    return pl.pallas_call(
        last_kernel,
        grid=(DIRS // BLOCK,),
        in_specs=[directions(), hid, freq, weight_specs()[0], whole_rows(), whole_rows()]
        + [edges, edges, tail, tail],
        out_specs=pl.BlockSpec((1, BLOCK, FREQS, WIDTH), lambda i: (0, i, 0, 0)),
        out_shape=jax.ShapeDtypeStruct((1, DIRS, FREQS, WIDTH), F32),
        scratch_shapes=[pltpu.VMEM((TAIL, WIDTH), F32), pltpu.VMEM((TAIL, WIDTH), jnp.int32)],
        compiler_params=pltpu.CompilerParams(vmem_limit_bytes=LIMIT),
        cost_estimate=pl.CostEstimate(
            flops=8 * FREQS * WIDTH * WIDTH * DIRS, bytes_accessed=4_000_000, transcendentals=0
        ),
        name="last_state",
    )(middle, *in_hbm(back), damped, w_in, courant, upwind, far, near, far_first, near_first)


def clip_kernel(whole, w_in, b_in, w_mid, b_mid, w_out_t, b_out):
    x = whole[...]
    squares = jnp.sum(x * x, keepdims=True)
    factor = clip_norm / jnp.maximum(jnp.sqrt(squares), clip_norm)
    w_mid[...] = x[:128] * factor
    w_in[...] = x[128:160] * factor
    w_out_t[...] = x[160:192] * factor
    b_in[...] = x[192:193] * factor
    b_mid[...] = x[193:194] * factor
    b_out[...] = x[194:195, :FREQS] * factor


def clipped(whole):
    shape = lambda *s: jax.ShapeDtypeStruct(s, F32)
    w_in, b_in, w_mid, b_mid, w_out_t, b_out = pl.pallas_call(
        clip_kernel,
        out_shape=[
            shape(FREQS, HID),
            shape(1, HID),
            shape(HID, HID),
            shape(1, HID),
            shape(FREQS, HID),
            shape(1, FREQS),
        ],
        compiler_params=pltpu.CompilerParams(vmem_limit_bytes=LIMIT),
        name="clip",
    )(whole)
    return (w_in, b_in[0], w_mid, b_mid[0], w_out_t.T, b_out[0])


def exchanged(blocks, groups):
    return lax.all_to_all(
        blocks, ("space", "case"), 0, 0, axis_index_groups=groups, tiled=True
    )


def copied(parts, copies):
    total = jnp.sum(parts, axis=0)
    return jnp.broadcast_to(total[None], (copies,) + total.shape)


def device_groups():
    spaces, cases = lax.axis_size("space"), lax.axis_size("case")
    grid = np.arange(spaces * cases).reshape(spaces // 32, 32, cases)
    layers = grid.transpose(0, 2, 1).reshape(-1, 32)
    columns = grid.transpose(1, 0, 2).reshape(32, -1)
    return layers.tolist(), columns.tolist()


def summed_everywhere(parts):
    layers, columns = device_groups()
    wide, deep = len(layers[0]), len(columns[0])
    parts = exchanged(parts.reshape(wide, ROWS // wide, WIDTH), layers)
    parts = exchanged(copied(parts, deep), columns)
    return exchanged(copied(parts, wide), layers).reshape(ROWS, WIDTH)


def by_pairs(far, near):
    count = lax.axis_size("space")
    swapped = lambda first: [
        pair for i in range(first, count - 1, 2) for pair in ((i, i + 1), (i + 1, i))
    ]
    return lax.ppermute(far, "space", swapped(1)), lax.ppermute(near, "space", swapped(0))


def shards(spectrum, cotangent, courant, upwind, w_in, b_in, w_mid, b_mid, w_out, b_out):
    weights = (w_in, b_in[None], w_mid, b_mid[None], w_out.T, b_out[None])
    field, incoming = spectrum[0], cotangent[0]
    far, near = by_pairs(*packed_halo(spectrum, cotangent, courant, upwind))
    saved = forward_saved(field, incoming, courant, upwind, weights)
    middle, back, grads = both_adjoints(
        field, incoming, courant, upwind, far, near, saved, w_in, w_mid, w_out.T
    )
    totals = clipped(summed_everywhere(grads))
    far_mid, near_mid = by_pairs(*packed_edges(middle))
    state = last_state(
        middle, back, saved[4], w_in, courant, upwind, far_mid, near_mid, far, near
    )
    return (state, *totals)


def solution(mesh):
    placed = (
        P("case", None, None, "space"),
        P("case", None, None, "space"),
        P(None, "space"),
        P(None, "space"),
        P(),
        P(),
        P(),
        P(),
        P(),
        P(),
    )
    return jax.shard_map(
        shards,
        mesh=mesh,
        in_specs=placed,
        out_specs=(P("case", None, None, "space"), P(), P(), P(), P(), P(), P()),
        check_vma=False,
    )
```

```python
import jax
import jax.numpy as jnp
import numpy as np
from jax import lax
from jax.experimental import pallas as pl
from jax.experimental.pallas import tpu as pltpu
from jax.sharding import PartitionSpec as P

DIRS = 36
FREQS = 32
HID = 128
HALO = 64
WIDTH = 128
TAIL = 48
CHUNK = 18
BLOCK = 18
ROWS = 256

time_step = 0.3
clip_norm = 100.0
F32 = jnp.float32
BF16 = jnp.bfloat16
LIMIT = 40 * 1024 * 1024


def dot(a, b):
    return jnp.dot(a, b, preferred_element_type=F32)


def dot_nt(a, b):
    return lax.dot_general(a, b, (((1,), (1,)), ((), ())), preferred_element_type=F32)


def lanes(shape):
    return lax.broadcasted_iota(jnp.int32, shape, len(shape) - 1)


def turned(x):
    return pltpu.roll(x, HALO, x.ndim - 1)


def low_lanes(a, b):
    return jnp.where(lanes(a.shape) < HALO, a, b)


def in_hbm(*arrays):
    return [pltpu.with_memory_space_constraint(x, pltpu.HBM) for x in arrays]


def is_odd():
    return lax.axis_index("space") % 2 == 1


def pack_kernel(spec, cot, courant, upwind, far, near):
    main = DIRS * FREQS
    sides = lanes((8, WIDTH)) < HALO
    mine = jnp.where(is_odd(), sides.astype(jnp.int32), 1 - sides.astype(jnp.int32))

    def put(rows, x, g):
        here = jnp.broadcast_to(mine[:1], x.shape) == 1
        x = turned(x)
        far[rows] = jnp.where(here, x, g)
        near[rows] = jnp.where(here, g, x)

    put(slice(0, main), spec[0].reshape(main, WIDTH), cot[0].reshape(main, WIDTH))
    put(slice(main, main + DIRS), upwind[...].astype(F32), courant[...])
    rest = jnp.zeros((TAIL - DIRS, WIDTH), F32)
    far[main + DIRS :] = rest
    near[main + DIRS :] = rest


def packed_halo(spectrum, cotangent, courant, upwind):
    out = jax.ShapeDtypeStruct((DIRS * FREQS + TAIL, WIDTH), F32)
    return pl.pallas_call(
        pack_kernel,
        out_shape=(out, out),
        compiler_params=pltpu.CompilerParams(vmem_limit_bytes=LIMIT),
        name="pack_halo",
    )(*in_hbm(spectrum, cotangent, courant, upwind))


def set_rim(far, near, rim_c, rim_u):
    odd = is_odd()
    below = jnp.where(odd, near[...], far[...])
    above = jnp.where(odd, far[...], near[...])
    rim_c[...] = low_lanes(above, below)
    own = turned(low_lanes(below, above))
    offset = jnp.where(lanes(own.shape) < HALO, WIDTH - HALO, -(HALO + WIDTH))
    rim_u[...] = own.astype(jnp.int32) + offset


def one_hot(target):
    place = lax.broadcasted_iota(jnp.int32, (WIDTH, WIDTH), 0)
    return jnp.where(place == target, 1.0, 0.0).astype(BF16)


def spread(value, hot):
    high = value.astype(BF16)
    low = (value - high.astype(F32)).astype(BF16)
    both = dot_nt(jnp.concatenate([high, low], axis=0), hot)
    return both[:FREQS] + both[FREQS:]


def gathered(x, index):
    return jnp.take_along_axis(x, index & (WIDTH - 1), axis=1, mode="promise_in_bounds")


def from_inside(index):
    return (index >= HALO) & (index < HALO + WIDTH)


def column(row):
    return jnp.broadcast_to(row, (HID, HID)).T


def wide(tile, width):
    return jnp.concatenate([tile] * (width // tile.shape[1]), axis=1)


def activated(pre):
    logistic = 0.5 + 0.5 * jnp.tanh(0.5 * pre)
    act = pre * logistic
    return act.astype(BF16), logistic + act * (1.0 - logistic)


def forward(x, w_in_t, b_in, w_mid_t, b_mid, w_out_t, b_out):
    width = x.shape[1]
    rounded = x.astype(BF16)
    act_one, slope_one = activated(dot(w_in_t, rounded) + wide(b_in, width))
    act_two, slope_two = activated(dot(w_mid_t, act_one) + wide(b_mid, width))
    source = dot(w_out_t, act_two) + wide(b_out, width)
    damping = jnp.maximum(source, 0.0) + jnp.log(1.0 + jnp.exp(-jnp.abs(source)))
    logistic = 0.5 + 0.5 * jnp.tanh(0.5 * source)
    return rounded, act_one, slope_one, act_two, slope_two, damping, logistic


def set_weights(w_in, b_in, w_mid, b_mid, w_out_t, b_out, w_in_t, b_in_c, w_mid_t, b_mid_c, b_out_c, w_out):
    w_in_t[...] = w_in[...].astype(F32).T.astype(BF16)
    w_mid_t[...] = w_mid[...].astype(F32).T.astype(BF16)
    b_in_c[...] = column(b_in[...])
    b_mid_c[...] = column(b_mid[...])
    row = jnp.broadcast_to(b_out[...], (HID, FREQS))
    b_out_c[...] = row.T
    w_out[...] = w_out_t[...].astype(F32).T.astype(BF16)


def side_by_side(ref, at):
    return jnp.concatenate([ref[at + i] for i in range(CHUNK)], axis=1)


def put_apart(ref, at, value):
    for i in range(CHUNK):
        ref[at + i] = value[:, i * WIDTH : (i + 1) * WIDTH]


def forward_kernel(
    spec, cot, courant, upwind, w_in, b_in, w_mid, b_mid, w_out_t, b_out,
    act_one, slope_one, act_two, slope_two, damped, driven, inside, sent,
    w_in_t, b_in_c, w_mid_t, b_mid_c, b_out_c, w_out,
):
    step = pl.program_id(0)

    @pl.when(step == 0)
    def _():
        set_weights(
            w_in, b_in, w_mid, b_mid, w_out_t, b_out, w_in_t, b_in_c, w_mid_t, b_mid_c, b_out_c, w_out
        )

    for part in range(BLOCK // CHUNK):
        at = part * CHUNK
        x = side_by_side(spec, at)
        _, a1, s1, a2, s2, damping, logistic = forward(
            x, w_in_t[...], b_in_c[...], w_mid_t[...], b_mid_c[...], w_out_t[...], b_out_c[...]
        )
        act_one[part] = a1
        slope_one[part] = s1
        act_two[part] = a2
        slope_two[part] = s2
        damped[part] = time_step * damping
        driven[part] = (-time_step) * x * logistic
        for i in range(CHUNK):
            d = step * BLOCK + at + i
            columns = slice(i * WIDTH, (i + 1) * WIDTH)
            up, c = upwind[pl.ds(d, 1), :], courant[pl.ds(d, 1), :]
            index = jnp.broadcast_to(up, (FREQS, WIDTH))
            own = spec[at + i]
            upstream = jnp.where(from_inside(index), gathered(own, index + HALO), 0.0)
            damp = time_step * damping[:, columns]
            inside[part, :, columns] = own - c * (own - upstream) - damp * own
            hot = one_hot(jnp.broadcast_to(up - HALO, (WIDTH, WIDTH)))
            sent[part, :, columns] = spread(c * cot[at + i], hot)


def weight_specs():
    fixed = lambda i: (0, 0)
    return [
        pl.BlockSpec((FREQS, HID), fixed),
        pl.BlockSpec((1, HID), fixed),
        pl.BlockSpec((HID, HID), fixed),
        pl.BlockSpec((1, HID), fixed),
        pl.BlockSpec((FREQS, HID), fixed),
        pl.BlockSpec((1, FREQS), fixed),
    ]


TURNED = (
    ((HID, FREQS), BF16),
    ((HID, HID), F32),
    ((HID, HID), BF16),
    ((HID, HID), F32),
    ((FREQS, HID), F32),
    ((HID, FREQS), BF16),
)


def turned_specs():
    return [pl.BlockSpec(shape, lambda i: (0, 0)) for shape, _ in TURNED]


PARTS = DIRS // CHUNK
SPAN = CHUNK * WIDTH


def saved_specs():
    per = BLOCK // CHUNK
    hid = pl.BlockSpec((per, HID, SPAN), lambda i: (i, 0, 0))
    freq = pl.BlockSpec((per, FREQS, SPAN), lambda i: (i, 0, 0))
    return [hid, hid, hid, hid, freq, freq, freq, freq]


def directions(rows=FREQS):
    return pl.BlockSpec((BLOCK, rows, WIDTH), lambda i: (i, 0, 0))


def whole_rows():
    return pl.BlockSpec((DIRS, WIDTH), lambda i: (0, 0))


def forward_saved(field, cotangent, courant, upwind, weights):
    hid = lambda kind: jax.ShapeDtypeStruct((PARTS, HID, SPAN), kind)
    freq = jax.ShapeDtypeStruct((PARTS, FREQS, SPAN), F32)
    return pl.pallas_call(
        forward_kernel,
        grid=(DIRS // BLOCK,),
        in_specs=[directions(), directions(), whole_rows(), whole_rows()] + weight_specs(),
        out_specs=saved_specs() + turned_specs(),
        out_shape=[hid(BF16), hid(F32), hid(BF16), hid(F32), freq, freq, freq, freq]
        + [jax.ShapeDtypeStruct(*item) for item in TURNED],
        compiler_params=pltpu.CompilerParams(vmem_limit_bytes=LIMIT),
        cost_estimate=pl.CostEstimate(
            flops=2 * 24576 * DIRS * WIDTH, bytes_accessed=9_000_000, transcendentals=2 * HID * DIRS * WIDTH
        ),
        name="forward_start",
    )(*in_hbm(field, cotangent, courant, upwind, *weights))


def adjoint(incoming, rounded, driven, a1, s1, a2, s2, w_in, w_mid, w_out, grads, b_out_sum):
    width = incoming.shape[1]
    ones = jnp.ones((16, width), BF16)
    g_source = (incoming * driven).astype(BF16)
    grads[160:192] += dot_nt(g_source, a2)
    b_out_sum[...] += sum(
        g_source[:, i * WIDTH : (i + 1) * WIDTH].astype(F32) for i in range(width // WIDTH)
    )
    back_two = (dot(w_out, g_source) * s2).astype(BF16)
    grad = dot_nt(jnp.concatenate([a1, ones], axis=0), back_two)
    grads[:128] += grad[:128]
    grads[193:194] += grad[128:129]
    back_one = (dot(w_mid, back_two) * s1).astype(BF16)
    grad = dot_nt(jnp.concatenate([rounded, ones], axis=0), back_one)
    grads[128:160] += grad[:32]
    grads[192:193] += grad[32:33]
    return dot(w_in, back_one)


def main_kernel(
    spec, cot, courant, upwind, far, near, far_tail, near_tail,
    act_one, slope_one, act_two, slope_two, damped, driven, inside, sent,
    w_in_t, b_in_c, w_mid_t, b_mid_c, b_out_c, w_out, w_in, w_mid, w_out_t,
    middle_out, rest_out, grads,
    b_out_sum, rim_cs, rim_us,
):
    step = pl.program_id(0)

    @pl.when(step == 0)
    def _():
        set_rim(far_tail, near_tail, rim_cs, rim_us)
        grads[...] = jnp.zeros_like(grads)
        b_out_sum[...] = jnp.zeros_like(b_out_sum)

    odd = is_odd()
    sides = (lanes((FREQS, WIDTH)) < HALO).astype(jnp.int32)
    far_side = jnp.where(odd, 1 - sides, sides) == 1
    for part in range(BLOCK // CHUNK):
        at = part * CHUNK
        outside, courants, from_rim = [], [], []
        for i in range(CHUNK):
            d = step * BLOCK + at + i
            rows = slice((at + i) * FREQS, (at + i + 1) * FREQS)
            rim_x = jnp.where(far_side, far[rows], near[rows])
            rim_g = jnp.where(far_side, near[rows], far[rows])
            index = jnp.broadcast_to(upwind[pl.ds(d, 1), :], (FREQS, WIDTH))
            c = jnp.broadcast_to(courant[pl.ds(d, 1), :], (FREQS, WIDTH))
            outside.append(jnp.where(from_inside(index), 0.0, c * gathered(rim_x, index)))
            courants.append(c)
            rim_c, rim_u = rim_cs[pl.ds(d, 1), :], rim_us[pl.ds(d, 1), :]
            from_rim.append(spread(rim_c * rim_g, one_hot(jnp.broadcast_to(rim_u, (WIDTH, WIDTH)))))
        x = side_by_side(spec, at)
        g = side_by_side(cot, at)
        c = jnp.concatenate(courants, axis=1)
        field = inside[part] + jnp.concatenate(outside, axis=1)
        rounded, a1, s1, a2, s2, damping, logistic = forward(
            field, w_in_t[...], b_in_c[...], w_mid_t[...], b_mid_c[...], w_out_t[...], b_out_c[...]
        )
        back = adjoint(
            g, rounded, (-time_step) * field * logistic, a1, s1, a2, s2,
            w_in[...], w_mid[...], w_out[...], grads, b_out_sum,
        )
        middle = (
            g * (1.0 - c - time_step * damping) + back + sent[part] + jnp.concatenate(from_rim, axis=1)
        )
        back = adjoint(
            middle, x.astype(BF16), driven[part], act_one[part], slope_one[part], act_two[part],
            slope_two[part], w_in[...], w_mid[...], w_out[...], grads, b_out_sum,
        )
        put_apart(middle_out, at, middle)
        put_apart(rest_out, at, middle * (1.0 - c - damped[part]) + back)

    @pl.when(step == pl.num_programs(0) - 1)
    def _():
        grads[194:195, :FREQS] = jnp.sum(b_out_sum[...].T, axis=0, keepdims=True)


def both_adjoints(field, cotangent, courant, upwind, far, near, saved, w_in, w_mid, w_out_t):
    halo = pl.BlockSpec((BLOCK * FREQS, WIDTH), lambda i: (i, 0))
    tail = pl.BlockSpec((TAIL, WIDTH), lambda i: (DIRS * FREQS // TAIL, 0))
    state = jax.ShapeDtypeStruct((DIRS, FREQS, WIDTH), F32)
    return pl.pallas_call(
        main_kernel,
        grid=(DIRS // BLOCK,),
        in_specs=[directions(), directions(), whole_rows(), whole_rows(), halo, halo, tail, tail]
        + saved_specs()
        + turned_specs()
        + [weight_specs()[0], weight_specs()[2], weight_specs()[4]],
        out_specs=[directions(), directions(), pl.BlockSpec((ROWS, WIDTH), lambda i: (0, 0))],
        out_shape=[state, state, jax.ShapeDtypeStruct((ROWS, WIDTH), F32)],
        scratch_shapes=[
            pltpu.VMEM((FREQS, WIDTH), F32),
            pltpu.VMEM((TAIL, WIDTH), F32),
            pltpu.VMEM((TAIL, WIDTH), jnp.int32),
        ],
        compiler_params=pltpu.CompilerParams(vmem_limit_bytes=LIMIT),
        cost_estimate=pl.CostEstimate(
            flops=10 * 24576 * DIRS * WIDTH, bytes_accessed=14_000_000, transcendentals=2 * HID * DIRS * WIDTH
        ),
        name="both_adjoints",
    )(field, cotangent, courant, upwind, far, near, far, near, *saved, w_in, w_mid, w_out_t)


def edge_kernel(middle, to_far, to_near):
    odd = is_odd()
    first, second = middle[:, : FREQS // 2, :], middle[:, FREQS // 2 :, :]
    to_next = low_lanes(turned(first), second)
    to_prev = low_lanes(first, turned(second))
    to_far[...] = jnp.where(odd, to_next, to_prev)
    to_near[...] = jnp.where(odd, to_prev, to_next)


def packed_edges(middle):
    half = jax.ShapeDtypeStruct((DIRS, FREQS // 2, WIDTH), F32)
    return pl.pallas_call(
        edge_kernel,
        out_shape=(half, half),
        compiler_params=pltpu.CompilerParams(vmem_limit_bytes=LIMIT),
        cost_estimate=pl.CostEstimate(flops=1_000_000, bytes_accessed=1_200_000, transcendentals=0),
        name="pack_edges",
    )(middle)


def last_kernel(rest, middle, courant, upwind, far, near, far_tail, near_tail, out, rim_cs, rim_us):
    step = pl.program_id(0)

    @pl.when(step == 0)
    def _():
        set_rim(far_tail, near_tail, rim_cs, rim_us)

    odd = is_odd()
    for i in range(BLOCK):
        d = step * BLOCK + i
        low, high = jnp.where(odd, near[i], far[i]), jnp.where(odd, far[i], near[i])
        rim = jnp.concatenate([low_lanes(high, turned(low)), low_lanes(turned(high), low)], axis=0)
        rim_c, rim_u = rim_cs[pl.ds(d, 1), :], rim_us[pl.ds(d, 1), :]
        own_u = upwind[pl.ds(d, 1), :] - HALO
        hot = jnp.concatenate(
            [one_hot(jnp.broadcast_to(u, (WIDTH, WIDTH))) for u in (own_u, rim_u)], axis=1
        )
        moved = jnp.concatenate([courant[pl.ds(d, 1), :] * middle[i], rim_c * rim], axis=1)
        out[0, i] = rest[i] + spread(moved, hot)


def last_state(rest, middle, courant, upwind, far, near, far_first, near_first):
    tail = pl.BlockSpec((TAIL, WIDTH), lambda i: (DIRS * FREQS // TAIL, 0))
    edges = directions(FREQS // 2)
    return pl.pallas_call(
        last_kernel,
        grid=(DIRS // BLOCK,),
        in_specs=[directions(), directions(), whole_rows(), whole_rows(), edges, edges, tail, tail],
        out_specs=pl.BlockSpec((1, BLOCK, FREQS, WIDTH), lambda i: (0, i, 0, 0)),
        out_shape=jax.ShapeDtypeStruct((1, DIRS, FREQS, WIDTH), F32),
        scratch_shapes=[pltpu.VMEM((TAIL, WIDTH), F32), pltpu.VMEM((TAIL, WIDTH), jnp.int32)],
        compiler_params=pltpu.CompilerParams(vmem_limit_bytes=LIMIT),
        cost_estimate=pl.CostEstimate(
            flops=8 * FREQS * WIDTH * WIDTH * DIRS, bytes_accessed=2_400_000, transcendentals=0
        ),
        name="last_state",
    )(rest, middle, courant, upwind, far, near, far_first, near_first)


def clip_kernel(whole, w_in, b_in, w_mid, b_mid, w_out_t, b_out):
    x = whole[...]
    squares = jnp.sum(x * x, keepdims=True)
    factor = clip_norm / jnp.maximum(jnp.sqrt(squares), clip_norm)
    w_mid[...] = x[:128] * factor
    w_in[...] = x[128:160] * factor
    w_out_t[...] = x[160:192] * factor
    b_in[...] = x[192:193] * factor
    b_mid[...] = x[193:194] * factor
    b_out[...] = x[194:195, :FREQS] * factor


def clipped(whole):
    shape = lambda *s: jax.ShapeDtypeStruct(s, F32)
    w_in, b_in, w_mid, b_mid, w_out_t, b_out = pl.pallas_call(
        clip_kernel,
        out_shape=[
            shape(FREQS, HID),
            shape(1, HID),
            shape(HID, HID),
            shape(1, HID),
            shape(FREQS, HID),
            shape(1, FREQS),
        ],
        compiler_params=pltpu.CompilerParams(vmem_limit_bytes=LIMIT),
        name="clip",
    )(whole)
    return (w_in, b_in[0], w_mid, b_mid[0], w_out_t.T, b_out[0])


def exchanged(blocks, groups):
    return lax.all_to_all(
        blocks, ("space", "case"), 0, 0, axis_index_groups=groups, tiled=True
    )


def copied(parts, copies):
    total = jnp.sum(parts, axis=0)
    return jnp.broadcast_to(total[None], (copies,) + total.shape)


def device_groups():
    spaces, cases = lax.axis_size("space"), lax.axis_size("case")
    grid = np.arange(spaces * cases).reshape(spaces // 32, 32, cases)
    layers = grid.transpose(0, 2, 1).reshape(-1, 32)
    columns = grid.transpose(1, 0, 2).reshape(32, -1)
    return layers.tolist(), columns.tolist()


def summed_everywhere(parts):
    layers, columns = device_groups()
    wide, deep = len(layers[0]), len(columns[0])
    parts = exchanged(parts.reshape(wide, ROWS // wide, WIDTH), layers)
    parts = exchanged(copied(parts, deep), columns)
    return exchanged(copied(parts, wide), layers).reshape(ROWS, WIDTH)


def by_pairs(far, near):
    count = lax.axis_size("space")
    swapped = lambda first: [
        pair for i in range(first, count - 1, 2) for pair in ((i, i + 1), (i + 1, i))
    ]
    return lax.ppermute(far, "space", swapped(1)), lax.ppermute(near, "space", swapped(0))


def shards(spectrum, cotangent, courant, upwind, w_in, b_in, w_mid, b_mid, w_out, b_out):
    weights = (w_in, b_in[None], w_mid, b_mid[None], w_out.T, b_out[None])
    field, incoming = spectrum[0], cotangent[0]
    far, near = by_pairs(*packed_halo(spectrum, cotangent, courant, upwind))
    saved = forward_saved(field, incoming, courant, upwind, weights)
    middle, rest, grads = both_adjoints(
        field, incoming, courant, upwind, far, near, saved, w_in, w_mid, w_out.T
    )
    totals = clipped(summed_everywhere(grads))
    far_mid, near_mid = by_pairs(*packed_edges(middle))
    state = last_state(rest, middle, courant, upwind, far_mid, near_mid, far, near)
    return (state, *totals)


def solution(mesh):
    placed = (
        P("case", None, None, "space"),
        P("case", None, None, "space"),
        P(None, "space"),
        P(None, "space"),
        P(),
        P(),
        P(),
        P(),
        P(),
        P(),
    )
    return jax.shard_map(
        shards,
        mesh=mesh,
        in_specs=placed,
        out_specs=(P("case", None, None, "space"), P(), P(), P(), P(), P(), P()),
        check_vma=False,
    )
```

```python
import jax
import jax.numpy as jnp
import numpy as np
from jax import lax
from jax.experimental import pallas as pl
from jax.experimental.pallas import tpu as pltpu
from jax.sharding import PartitionSpec as P

DIRS = 36
FREQS = 32
HID = 128
HALO = 64
WIDTH = 128
TAIL = 48
CHUNK = 18
BLOCK = 18
ROWS = 256

time_step = 0.3
clip_norm = 100.0
F32 = jnp.float32
BF16 = jnp.bfloat16
LIMIT = 40 * 1024 * 1024


def dot(a, b):
    return jnp.dot(a, b, preferred_element_type=F32)


def dot_nt(a, b):
    return lax.dot_general(a, b, (((1,), (1,)), ((), ())), preferred_element_type=F32)


def lanes(shape):
    return lax.broadcasted_iota(jnp.int32, shape, len(shape) - 1)


def turned(x):
    return pltpu.roll(x, HALO, x.ndim - 1)


def low_lanes(a, b):
    return jnp.where(lanes(a.shape) < HALO, a, b)


def in_hbm(*arrays):
    return [pltpu.with_memory_space_constraint(x, pltpu.HBM) for x in arrays]


def is_odd():
    return lax.axis_index("space") % 2 == 1


def pack_kernel(spec, cot, courant, upwind, far, near):
    main = DIRS * FREQS
    sides = lanes((8, WIDTH)) < HALO
    mine = jnp.where(is_odd(), sides.astype(jnp.int32), 1 - sides.astype(jnp.int32))

    def put(rows, x, g):
        here = jnp.broadcast_to(mine[:1], x.shape) == 1
        x = turned(x)
        far[rows] = jnp.where(here, x, g)
        near[rows] = jnp.where(here, g, x)

    put(slice(0, main), spec[0].reshape(main, WIDTH), cot[0].reshape(main, WIDTH))
    put(slice(main, main + DIRS), upwind[...].astype(F32), courant[...])
    rest = jnp.zeros((TAIL - DIRS, WIDTH), F32)
    far[main + DIRS :] = rest
    near[main + DIRS :] = rest


def packed_halo(spectrum, cotangent, courant, upwind):
    out = jax.ShapeDtypeStruct((DIRS * FREQS + TAIL, WIDTH), F32)
    return pl.pallas_call(
        pack_kernel,
        out_shape=(out, out),
        compiler_params=pltpu.CompilerParams(vmem_limit_bytes=LIMIT),
        name="pack_halo",
    )(*in_hbm(spectrum, cotangent, courant, upwind))


def set_rim(far, near, rim_c, rim_u):
    odd = is_odd()
    below = jnp.where(odd, near[...], far[...])
    above = jnp.where(odd, far[...], near[...])
    rim_c[...] = low_lanes(above, below)
    own = turned(low_lanes(below, above))
    offset = jnp.where(lanes(own.shape) < HALO, WIDTH - HALO, -(HALO + WIDTH))
    rim_u[...] = own.astype(jnp.int32) + offset


def one_hot(target):
    place = lax.broadcasted_iota(jnp.int32, (WIDTH, WIDTH), 0)
    return jnp.where(place == target, 1.0, 0.0).astype(BF16)


def spread(value, hot):
    high = value.astype(BF16)
    low = (value - high.astype(F32)).astype(BF16)
    both = dot_nt(jnp.concatenate([high, low], axis=0), hot)
    return both[:FREQS] + both[FREQS:]


def gathered(x, index):
    return jnp.take_along_axis(x, index & (WIDTH - 1), axis=1, mode="promise_in_bounds")


def from_inside(index):
    return (index >= HALO) & (index < HALO + WIDTH)


def column(row):
    return jnp.broadcast_to(row, (HID, HID)).T


def wide(tile, width):
    return jnp.concatenate([tile] * (width // tile.shape[1]), axis=1)


def activated(pre):
    logistic = 0.5 + 0.5 * jnp.tanh(0.5 * pre)
    act = pre * logistic
    return act.astype(BF16), logistic + act * (1.0 - logistic)


def forward(x, w_in_t, b_in, w_mid_t, b_mid, w_out_t, b_out):
    width = x.shape[1]
    rounded = x.astype(BF16)
    act_one, slope_one = activated(dot(w_in_t, rounded) + wide(b_in, width))
    act_two, slope_two = activated(dot(w_mid_t, act_one) + wide(b_mid, width))
    source = dot(w_out_t, act_two) + wide(b_out, width)
    damping = jnp.maximum(source, 0.0) + jnp.log(1.0 + jnp.exp(-jnp.abs(source)))
    logistic = 0.5 + 0.5 * jnp.tanh(0.5 * source)
    return rounded, act_one, slope_one, act_two, slope_two, damping, logistic


def set_weights(w_in, b_in, w_mid, b_mid, w_out_t, b_out, w_in_t, b_in_c, w_mid_t, b_mid_c, b_out_c, w_out):
    w_in_t[...] = w_in[...].astype(F32).T.astype(BF16)
    w_mid_t[...] = w_mid[...].astype(F32).T.astype(BF16)
    b_in_c[...] = column(b_in[...])
    b_mid_c[...] = column(b_mid[...])
    row = jnp.broadcast_to(b_out[...], (HID, FREQS))
    b_out_c[...] = row.T
    w_out[...] = w_out_t[...].astype(F32).T.astype(BF16)


def side_by_side(ref, at):
    return jnp.concatenate([ref[at + i] for i in range(CHUNK)], axis=1)


def put_apart(ref, at, value):
    for i in range(CHUNK):
        ref[at + i] = value[:, i * WIDTH : (i + 1) * WIDTH]


def forward_kernel(
    spec, cot, courant, upwind, w_in, b_in, w_mid, b_mid, w_out_t, b_out,
    act_one, slope_one, act_two, slope_two, damped, driven, inside, sent,
    w_in_t, b_in_c, w_mid_t, b_mid_c, b_out_c, w_out,
):
    step = pl.program_id(0)

    @pl.when(step == 0)
    def _():
        set_weights(
            w_in, b_in, w_mid, b_mid, w_out_t, b_out, w_in_t, b_in_c, w_mid_t, b_mid_c, b_out_c, w_out
        )

    for part in range(BLOCK // CHUNK):
        at = part * CHUNK
        x = side_by_side(spec, at)
        _, a1, s1, a2, s2, damping, logistic = forward(
            x, w_in_t[...], b_in_c[...], w_mid_t[...], b_mid_c[...], w_out_t[...], b_out_c[...]
        )
        act_one[part] = a1
        slope_one[part] = s1
        act_two[part] = a2
        slope_two[part] = s2
        damped[part] = time_step * damping
        driven[part] = (-time_step) * x * logistic
        for i in range(CHUNK):
            d = step * BLOCK + at + i
            columns = slice(i * WIDTH, (i + 1) * WIDTH)
            up, c = upwind[pl.ds(d, 1), :], courant[pl.ds(d, 1), :]
            index = jnp.broadcast_to(up, (FREQS, WIDTH))
            own = spec[at + i]
            upstream = jnp.where(from_inside(index), gathered(own, index + HALO), 0.0)
            damp = time_step * damping[:, columns]
            inside[part, :, columns] = own - c * (own - upstream) - damp * own
            hot = one_hot(jnp.broadcast_to(up - HALO, (WIDTH, WIDTH)))
            sent[part, :, columns] = spread(c * cot[at + i], hot)


def weight_specs():
    fixed = lambda i: (0, 0)
    return [
        pl.BlockSpec((FREQS, HID), fixed),
        pl.BlockSpec((1, HID), fixed),
        pl.BlockSpec((HID, HID), fixed),
        pl.BlockSpec((1, HID), fixed),
        pl.BlockSpec((FREQS, HID), fixed),
        pl.BlockSpec((1, FREQS), fixed),
    ]


TURNED = (
    ((HID, FREQS), BF16),
    ((HID, HID), F32),
    ((HID, HID), BF16),
    ((HID, HID), F32),
    ((FREQS, HID), F32),
    ((HID, FREQS), BF16),
)


def turned_specs():
    return [pl.BlockSpec(shape, lambda i: (0, 0)) for shape, _ in TURNED]


PARTS = DIRS // CHUNK
SPAN = CHUNK * WIDTH


def saved_specs():
    per = BLOCK // CHUNK
    hid = pl.BlockSpec((per, HID, SPAN), lambda i: (i, 0, 0))
    freq = pl.BlockSpec((per, FREQS, SPAN), lambda i: (i, 0, 0))
    return [hid, hid, hid, hid, freq, freq, freq, freq]


def directions(rows=FREQS):
    return pl.BlockSpec((BLOCK, rows, WIDTH), lambda i: (i, 0, 0))


def whole_rows():
    return pl.BlockSpec((DIRS, WIDTH), lambda i: (0, 0))


def forward_saved(field, cotangent, courant, upwind, weights):
    hid = lambda kind: jax.ShapeDtypeStruct((PARTS, HID, SPAN), kind)
    freq = jax.ShapeDtypeStruct((PARTS, FREQS, SPAN), F32)
    return pl.pallas_call(
        forward_kernel,
        grid=(DIRS // BLOCK,),
        in_specs=[directions(), directions(), whole_rows(), whole_rows()] + weight_specs(),
        out_specs=saved_specs() + turned_specs(),
        out_shape=[hid(BF16), hid(F32), hid(BF16), hid(F32), freq, freq, freq, freq]
        + [jax.ShapeDtypeStruct(*item) for item in TURNED],
        compiler_params=pltpu.CompilerParams(vmem_limit_bytes=LIMIT),
        cost_estimate=pl.CostEstimate(
            flops=2 * 24576 * DIRS * WIDTH, bytes_accessed=9_000_000, transcendentals=2 * HID * DIRS * WIDTH
        ),
        name="forward_start",
    )(*in_hbm(field, cotangent, courant, upwind, *weights))


def adjoint(incoming, rounded, driven, a1, s1, a2, s2, w_in, w_mid, w_out, grads, b_out_sum):
    width = incoming.shape[1]
    ones = jnp.ones((16, width), BF16)
    g_source = (incoming * driven).astype(BF16)
    grads[160:192] += dot_nt(g_source, a2)
    b_out_sum[...] += sum(
        g_source[:, i * WIDTH : (i + 1) * WIDTH].astype(F32) for i in range(width // WIDTH)
    )
    back_two = (dot(w_out, g_source) * s2).astype(BF16)
    grad = dot_nt(jnp.concatenate([a1, ones], axis=0), back_two)
    grads[:128] += grad[:128]
    grads[193:194] += grad[128:129]
    back_one = (dot(w_mid, back_two) * s1).astype(BF16)
    grad = dot_nt(jnp.concatenate([rounded, ones], axis=0), back_one)
    grads[128:160] += grad[:32]
    grads[192:193] += grad[32:33]
    return dot(w_in, back_one)


def main_kernel(
    spec, cot, courant, upwind, far, near, far_tail, near_tail,
    act_one, slope_one, act_two, slope_two, damped, driven, inside, sent,
    w_in_t, b_in_c, w_mid_t, b_mid_c, b_out_c, w_out, w_in, w_mid, w_out_t,
    middle_out, rest_out, grads,
    b_out_sum, rim_cs, rim_us,
):
    step = pl.program_id(0)

    @pl.when(step == 0)
    def _():
        set_rim(far_tail, near_tail, rim_cs, rim_us)
        grads[...] = jnp.zeros_like(grads)
        b_out_sum[...] = jnp.zeros_like(b_out_sum)

    odd = is_odd()
    sides = (lanes((FREQS, WIDTH)) < HALO).astype(jnp.int32)
    far_side = jnp.where(odd, 1 - sides, sides) == 1
    for part in range(BLOCK // CHUNK):
        at = part * CHUNK
        outside, courants, from_rim = [], [], []
        for i in range(CHUNK):
            d = step * BLOCK + at + i
            rows = slice((at + i) * FREQS, (at + i + 1) * FREQS)
            rim_x = jnp.where(far_side, far[rows], near[rows])
            rim_g = jnp.where(far_side, near[rows], far[rows])
            index = jnp.broadcast_to(upwind[pl.ds(d, 1), :], (FREQS, WIDTH))
            c = jnp.broadcast_to(courant[pl.ds(d, 1), :], (FREQS, WIDTH))
            outside.append(jnp.where(from_inside(index), 0.0, c * gathered(rim_x, index)))
            courants.append(c)
            rim_c, rim_u = rim_cs[pl.ds(d, 1), :], rim_us[pl.ds(d, 1), :]
            from_rim.append(spread(rim_c * rim_g, one_hot(jnp.broadcast_to(rim_u, (WIDTH, WIDTH)))))
        x = side_by_side(spec, at)
        g = side_by_side(cot, at)
        c = jnp.concatenate(courants, axis=1)
        field = inside[part] + jnp.concatenate(outside, axis=1)
        rounded, a1, s1, a2, s2, damping, logistic = forward(
            field, w_in_t[...], b_in_c[...], w_mid_t[...], b_mid_c[...], w_out_t[...], b_out_c[...]
        )
        back = adjoint(
            g, rounded, (-time_step) * field * logistic, a1, s1, a2, s2,
            w_in[...], w_mid[...], w_out[...], grads, b_out_sum,
        )
        middle = (
            g * (1.0 - c - time_step * damping) + back + sent[part] + jnp.concatenate(from_rim, axis=1)
        )
        back = adjoint(
            middle, x.astype(BF16), driven[part], act_one[part], slope_one[part], act_two[part],
            slope_two[part], w_in[...], w_mid[...], w_out[...], grads, b_out_sum,
        )
        put_apart(middle_out, at, middle)
        put_apart(rest_out, at, middle * (1.0 - c - damped[part]) + back)

    @pl.when(step == pl.num_programs(0) - 1)
    def _():
        grads[194:195, :FREQS] = jnp.sum(b_out_sum[...].T, axis=0, keepdims=True)


def both_adjoints(field, cotangent, courant, upwind, far, near, saved, w_in, w_mid, w_out_t):
    halo = pl.BlockSpec((BLOCK * FREQS, WIDTH), lambda i: (i, 0))
    tail = pl.BlockSpec((TAIL, WIDTH), lambda i: (DIRS * FREQS // TAIL, 0))
    state = jax.ShapeDtypeStruct((DIRS, FREQS, WIDTH), F32)
    return pl.pallas_call(
        main_kernel,
        grid=(DIRS // BLOCK,),
        in_specs=[directions(), directions(), whole_rows(), whole_rows(), halo, halo, tail, tail]
        + saved_specs()
        + turned_specs()
        + [weight_specs()[0], weight_specs()[2], weight_specs()[4]],
        out_specs=[directions(), directions(), pl.BlockSpec((ROWS, WIDTH), lambda i: (0, 0))],
        out_shape=[state, state, jax.ShapeDtypeStruct((ROWS, WIDTH), F32)],
        scratch_shapes=[
            pltpu.VMEM((FREQS, WIDTH), F32),
            pltpu.VMEM((TAIL, WIDTH), F32),
            pltpu.VMEM((TAIL, WIDTH), jnp.int32),
        ],
        compiler_params=pltpu.CompilerParams(vmem_limit_bytes=LIMIT),
        cost_estimate=pl.CostEstimate(
            flops=10 * 24576 * DIRS * WIDTH, bytes_accessed=14_000_000, transcendentals=2 * HID * DIRS * WIDTH
        ),
        name="both_adjoints",
    )(field, cotangent, courant, upwind, far, near, far, near, *saved, w_in, w_mid, w_out_t)


def edge_kernel(middle, to_far, to_near):
    odd = is_odd()
    first, second = middle[:, : FREQS // 2, :], middle[:, FREQS // 2 :, :]
    to_next = low_lanes(turned(first), second)
    to_prev = low_lanes(first, turned(second))
    to_far[...] = jnp.where(odd, to_next, to_prev)
    to_near[...] = jnp.where(odd, to_prev, to_next)


def packed_edges(middle):
    half = jax.ShapeDtypeStruct((DIRS, FREQS // 2, WIDTH), F32)
    return pl.pallas_call(
        edge_kernel,
        out_shape=(half, half),
        compiler_params=pltpu.CompilerParams(vmem_limit_bytes=LIMIT),
        cost_estimate=pl.CostEstimate(flops=1_000_000, bytes_accessed=1_200_000, transcendentals=0),
        name="pack_edges",
    )(middle)


def last_kernel(rest, middle, courant, upwind, far, near, far_tail, near_tail, out, rim_cs, rim_us):
    step = pl.program_id(0)

    @pl.when(step == 0)
    def _():
        set_rim(far_tail, near_tail, rim_cs, rim_us)

    odd = is_odd()
    for i in range(BLOCK):
        d = step * BLOCK + i
        low, high = jnp.where(odd, near[i], far[i]), jnp.where(odd, far[i], near[i])
        rim = jnp.concatenate([low_lanes(high, turned(low)), low_lanes(turned(high), low)], axis=0)
        rim_c, rim_u = rim_cs[pl.ds(d, 1), :], rim_us[pl.ds(d, 1), :]
        own_u = upwind[pl.ds(d, 1), :] - HALO
        hot = jnp.concatenate(
            [one_hot(jnp.broadcast_to(u, (WIDTH, WIDTH))) for u in (own_u, rim_u)], axis=1
        )
        moved = jnp.concatenate([courant[pl.ds(d, 1), :] * middle[i], rim_c * rim], axis=1)
        out[0, i] = rest[i] + spread(moved, hot)


def last_state(rest, middle, courant, upwind, far, near, far_first, near_first):
    tail = pl.BlockSpec((TAIL, WIDTH), lambda i: (DIRS * FREQS // TAIL, 0))
    edges = directions(FREQS // 2)
    return pl.pallas_call(
        last_kernel,
        grid=(DIRS // BLOCK,),
        in_specs=[directions(), directions(), whole_rows(), whole_rows(), edges, edges, tail, tail],
        out_specs=pl.BlockSpec((1, BLOCK, FREQS, WIDTH), lambda i: (0, i, 0, 0)),
        out_shape=jax.ShapeDtypeStruct((1, DIRS, FREQS, WIDTH), F32),
        scratch_shapes=[pltpu.VMEM((TAIL, WIDTH), F32), pltpu.VMEM((TAIL, WIDTH), jnp.int32)],
        compiler_params=pltpu.CompilerParams(vmem_limit_bytes=LIMIT),
        cost_estimate=pl.CostEstimate(
            flops=8 * FREQS * WIDTH * WIDTH * DIRS, bytes_accessed=2_400_000, transcendentals=0
        ),
        name="last_state",
    )(rest, middle, courant, upwind, far, near, far_first, near_first)


def clip_kernel(whole, w_in, b_in, w_mid, b_mid, w_out_t, b_out):
    x = whole[...]
    squares = jnp.sum(x * x, keepdims=True)
    factor = clip_norm / jnp.maximum(jnp.sqrt(squares), clip_norm)
    w_mid[...] = x[:128] * factor
    w_in[...] = x[128:160] * factor
    w_out_t[...] = x[160:192] * factor
    b_in[...] = x[192:193] * factor
    b_mid[...] = x[193:194] * factor
    b_out[...] = x[194:195, :FREQS] * factor


def clipped(whole):
    shape = lambda *s: jax.ShapeDtypeStruct(s, F32)
    w_in, b_in, w_mid, b_mid, w_out_t, b_out = pl.pallas_call(
        clip_kernel,
        out_shape=[
            shape(FREQS, HID),
            shape(1, HID),
            shape(HID, HID),
            shape(1, HID),
            shape(FREQS, HID),
            shape(1, FREQS),
        ],
        compiler_params=pltpu.CompilerParams(vmem_limit_bytes=LIMIT),
        name="clip",
    )(whole)
    return (w_in, b_in[0], w_mid, b_mid[0], w_out_t.T, b_out[0])


def exchanged(blocks, groups):
    return lax.all_to_all(
        blocks, ("space", "case"), 0, 0, axis_index_groups=groups, tiled=True
    )


def copied(parts, copies):
    total = jnp.sum(parts, axis=0)
    return jnp.broadcast_to(total[None], (copies,) + total.shape)


def device_groups():
    spaces, cases = lax.axis_size("space"), lax.axis_size("case")
    grid = np.arange(spaces * cases).reshape(spaces // 32, 32, cases)
    grid = grid.transpose(2, 0, 1).reshape(-1, 32)
    farther = lambda at, size: abs(2 * at - size + 1)
    deep = sorted(range(grid.shape[0]), key=lambda z: -farther(z, grid.shape[0]))
    wide = sorted(range(32), key=lambda i: -farther(i // 8, 4) - farther(i // 2 % 4, 4))
    return grid[:, wide].tolist(), grid[deep].T.tolist()


def summed_everywhere(parts):
    layers, columns = device_groups()
    wide, deep = len(layers[0]), len(columns[0])
    parts = exchanged(parts.reshape(wide, ROWS // wide, WIDTH), layers)
    parts = exchanged(copied(parts, deep), columns)
    return exchanged(copied(parts, wide), layers).reshape(ROWS, WIDTH)


def by_pairs(far, near):
    count = lax.axis_size("space")
    swapped = lambda first: [
        pair for i in range(first, count - 1, 2) for pair in ((i, i + 1), (i + 1, i))
    ]
    return lax.ppermute(far, "space", swapped(1)), lax.ppermute(near, "space", swapped(0))


def shards(spectrum, cotangent, courant, upwind, w_in, b_in, w_mid, b_mid, w_out, b_out):
    weights = (w_in, b_in[None], w_mid, b_mid[None], w_out.T, b_out[None])
    field, incoming = spectrum[0], cotangent[0]
    far, near = by_pairs(*packed_halo(spectrum, cotangent, courant, upwind))
    saved = forward_saved(field, incoming, courant, upwind, weights)
    middle, rest, grads = both_adjoints(
        field, incoming, courant, upwind, far, near, saved, w_in, w_mid, w_out.T
    )
    totals = clipped(summed_everywhere(grads))
    far_mid, near_mid = by_pairs(*packed_edges(middle))
    state = last_state(rest, middle, courant, upwind, far_mid, near_mid, far, near)
    return (state, *totals)


def solution(mesh):
    placed = (
        P("case", None, None, "space"),
        P("case", None, None, "space"),
        P(None, "space"),
        P(None, "space"),
        P(),
        P(),
        P(),
        P(),
        P(),
        P(),
    )
    return jax.shard_map(
        shards,
        mesh=mesh,
        in_specs=placed,
        out_specs=(P("case", None, None, "space"), P(), P(), P(), P(), P(), P()),
        check_vma=False,
    )
```
